32 devices in a mesh: row: 4 (over z), col: 8 (over y, x, core).
Axes of the slice: x: 2, y: 2, z: 4, core: 2. Of those that a mesh axis runs over, the one named last changes fastest.
Arguments:
- embed: bfloat16 [65536, 64], P(('row', 'col')), may hold values from -6 to 6
- tiles: bfloat16 [2048, 128, 128], P(('row', 'col'))
- tile_rows: int32 [2048], P(('row', 'col')), may hold values from 0 to 511, as said below
- tile_cols: int32 [2048], P(('row', 'col')), may hold values from 0 to 511, as said below
- chg_tiles: bfloat16 [1536, 128, 128], P(('row', 'col'))
- chg_rows: int32 [1536], P(('row', 'col')), may hold values from 0 to 511, as said below
- chg_cols: int32 [1536], P(('row', 'col')), may hold values from 0 to 511, as said below
Outputs:
- embedding: float32 [65536, 64], P(('row', 'col'))
The draws below stay inside these ranges and needn't reach their ends.
Inputs may be any that keep to these rules, and one draw needn't show every extreme that they name: Tile n lies in the row group of the device that holds it: tile_rows[n] // 128 equals (n // 64) // 8. Tile n lies in the column group of the device that holds it: tile_cols[n] // 64 equals (n // 64) % 8. `chg_rows`: one device's list names each transpose owner at most 3 times; in every draw some owner is named exactly 3 times by every device's list. `chg_cols`: read with chg_rows to give the transpose owner.
All inputs are finite; a program needn't handle non-finite values.
Results may differ from the reference program's by a relative error of at most 0.025.
Values may be sent and summed in bfloat16 or wider, within the bound.
No kernel may reach another device: no remote copies, remote signals or barrier semaphores. Data moves between devices by JAX's collectives and lax.ppermute only.
A program may use at most 192 MiB of HBM per device.

```python
import math
import jax
import jax.numpy as jnp
from jax import lax

K = 64
TILE = 128
ITERS = 3
CAP = 3
ROWS_DEV = 2048
TILES_DEV = 64
NODES = 65536
BLOCKS = 512
ROW_BLK = 128
COL_BLK = 64
COL_ROWS = 8192
SUB = 64
CHG_DEV = 48
N_ROW = 4
N_COL = 8
DEVICES = 32


def tile_values(key, count, groups):
    reach = 1.15
    spread = 1.0
    mean_size = 0.8 * (math.sinh(reach) / reach) ** 2
    along = TILES_DEV * TILE / ROWS_DEV + CAP * DEVICES * TILE / (2.0 * ROWS_DEV)
    base = 1.0 / (along * TILE * mean_size)
    levels = base * jnp.power(10.0, -spread * groups.astype(jnp.float32) / (N_ROW - 1))
    levels = levels.reshape(DEVICES, count)

    def one_device(inputs):
        device, level = inputs
        device_key = jax.random.fold_in(key, device)
        shape = (count, TILE, TILE)
        values = jax.random.normal(jax.random.fold_in(device_key, 1), shape, jnp.float32)
        row_scale = jnp.exp(jax.random.uniform(jax.random.fold_in(device_key, 2), (count, TILE, 1), jnp.float32, -reach, reach))
        col_scale = jnp.exp(jax.random.uniform(jax.random.fold_in(device_key, 3), (count, 1, TILE), jnp.float32, -reach, reach))
        return (values * row_scale * col_scale * level[:, None, None]).astype(jnp.bfloat16)
    blocks = lax.map(one_device, (jnp.arange(DEVICES, dtype=jnp.int32), levels))
    return blocks.reshape(DEVICES * count, TILE, TILE)


def draw_tiles(key, part):
    holder = jnp.arange(DEVICES * TILES_DEV, dtype=jnp.int32) // TILES_DEV
    return tile_values(jax.random.fold_in(key, 5), TILES_DEV, holder // N_COL)


def draw_chg_tiles(key, part):
    owners = owner_table(key)
    return tile_values(jax.random.fold_in(key, 6), CHG_DEV, owners // N_COL)


def draw_tile_rows(key, part):
    holder = jnp.arange(DEVICES * TILES_DEV, dtype=jnp.int32) // TILES_DEV
    offset = jax.random.randint(jax.random.fold_in(key, 21), (DEVICES * TILES_DEV,), 0, ROW_BLK, dtype=jnp.int32)
    return holder // N_COL * ROW_BLK + offset


def draw_tile_cols(key, part):
    holder = jnp.arange(DEVICES * TILES_DEV, dtype=jnp.int32) // TILES_DEV
    offset = jax.random.randint(jax.random.fold_in(key, 22), (DEVICES * TILES_DEV,), 0, COL_BLK, dtype=jnp.int32)
    return holder % N_COL * COL_BLK + offset


def owner_table(key):
    half_count = CHG_DEV // 2
    spare = half_count - 1
    rank_order = jnp.argsort(jax.random.permutation(jax.random.fold_in(key, 31), DEVICES)).astype(jnp.int32)
    extra_weight = jnp.where(rank_order == 0, 100 * DEVICES, jnp.where(rank_order < DEVICES // 8, 3 * DEVICES, 0))
    random_jitter = jax.random.randint(jax.random.fold_in(key, 32), (DEVICES, DEVICES), 0, 4 * DEVICES, dtype=jnp.int32)
    score_values = (random_jitter + extra_weight[None, :]) * DEVICES + jnp.arange(DEVICES, dtype=jnp.int32)[None, :]
    chosen = jnp.argsort(-score_values, axis=1)[:, :half_count].astype(jnp.int32)
    first_keys = jax.random.randint(jax.random.fold_in(key, 33), (DEVICES, spare), 0, 1 << 20, dtype=jnp.int32) * spare + jnp.arange(spare, dtype=jnp.int32)[None, :]
    second_keys = jax.random.randint(jax.random.fold_in(key, 34), (DEVICES, spare), 0, 1 << 20, dtype=jnp.int32) * spare + jnp.arange(spare, dtype=jnp.int32)[None, :]
    first_picks = jnp.argsort(first_keys, axis=1)[:, :half_count // 2 - 1].astype(jnp.int32) + 1
    second_picks = jnp.argsort(second_keys, axis=1)[:, :half_count // 2 - 1].astype(jnp.int32) + 1
    zero_pick = jnp.zeros((DEVICES, 1), jnp.int32)
    every_once = jnp.broadcast_to(jnp.arange(half_count, dtype=jnp.int32)[None, :], (DEVICES, half_count))
    picks = jnp.concatenate([every_once, zero_pick, first_picks, zero_pick, second_picks], axis=1)
    return jnp.take_along_axis(chosen, picks, axis=1).reshape(DEVICES * CHG_DEV)


def draw_chg_rows(key, part):
    owners = owner_table(key)
    offset = jax.random.randint(jax.random.fold_in(key, 41), (DEVICES * CHG_DEV,), 0, COL_BLK, dtype=jnp.int32)
    return owners % N_COL * COL_BLK + offset


def draw_chg_cols(key, part):
    owners = owner_table(key)
    offset = jax.random.randint(jax.random.fold_in(key, 42), (DEVICES * CHG_DEV,), 0, ROW_BLK, dtype=jnp.int32)
    return owners // N_COL * ROW_BLK + offset


def level_of(key, shape, split, low, high):
    loudness, own = 1.0, jax.random.fold_in(key, 6)
    for dim, parts in split:
        steps = jnp.exp(jax.random.uniform(jax.random.fold_in(own, dim), (parts,), jnp.float32, low / len(split), high / len(split)))
        loudness = loudness * jnp.repeat(steps, shape[dim] // parts).reshape([-1 if axis == dim else 1 for axis in range(len(shape))])
    return loudness


def bell_draw(stream_key, dims, width, bound, cuts=(), kind=jnp.bfloat16):
    array = width * jax.random.normal(stream_key, dims, jnp.float32)
    if cuts:
        array = array * level_of(stream_key, dims, cuts, -0.22, 0.18)
    return jnp.clip(array, -bound, bound).astype(kind)


def setup_inputs(seed: int = 0) -> dict:
    streams_of = jax.random.split(jax.random.key(seed), 8)
    embed = bell_draw(streams_of[0], (NODES, K), 1.0, 6.0, ((0, 32),))
    tiles = draw_tiles(jax.random.fold_in(streams_of[7], 71), 0)
    tile_rows = draw_tile_rows(jax.random.fold_in(streams_of[7], 71), 0)
    tile_cols = draw_tile_cols(jax.random.fold_in(streams_of[7], 71), 0)
    chg_tiles = draw_chg_tiles(jax.random.fold_in(streams_of[7], 71), 0)
    chg_rows = draw_chg_rows(jax.random.fold_in(streams_of[7], 71), 0)
    chg_cols = draw_chg_cols(jax.random.fold_in(streams_of[7], 71), 0)
    return {"embed": embed, "tiles": tiles, "tile_rows": tile_rows, "tile_cols": tile_cols, "chg_tiles": chg_tiles, "chg_rows": chg_rows, "chg_cols": chg_cols}


def column_order(vectors):
    feature_width = vectors.shape[1]
    pieces = vectors.reshape(DEVICES, N_ROW, N_COL, SUB, feature_width)
    return jnp.transpose(pieces, (2, 1, 0, 3, 4)).reshape(NODES, feature_width)

def mirror_table(chg_rows, chg_cols):
    owners = (chg_cols // ROW_BLK * N_COL + chg_rows // COL_BLK).astype(jnp.int32)
    listed = owners.reshape(DEVICES, CHG_DEV)
    position = jnp.arange(CHG_DEV, dtype=jnp.int32)
    earlier = position[None, :] < position[:, None]
    same_owner = listed[:, :, None] == listed[:, None, :]
    slot_rank = jnp.sum(jnp.logical_and(same_owner, earlier[None, :, :]), axis=2).astype(jnp.int32)
    entries = DEVICES * CHG_DEV
    sources = jnp.broadcast_to(jnp.arange(DEVICES, dtype=jnp.int32)[:, None], (DEVICES, CHG_DEV))
    numbers = jnp.arange(entries, dtype=jnp.int32).reshape(DEVICES, CHG_DEV)
    table = jnp.full((DEVICES, DEVICES * CAP), entries, jnp.int32)
    return table.at[listed, sources * CAP + slot_rank].set(numbers)

def reference(embed, tiles, tile_rows, tile_cols, chg_tiles, chg_rows, chg_cols):
    table = mirror_table(chg_rows, chg_cols)
    padded = jnp.concatenate([chg_tiles, jnp.zeros((1, TILE, TILE), chg_tiles.dtype)], axis=0)
    zero_index = jnp.zeros((1,), jnp.int32)
    mirror_rows = jnp.concatenate([(chg_cols % ROW_BLK).astype(jnp.int32), zero_index])
    mirror_cols = jnp.concatenate([(chg_rows % COL_BLK).astype(jnp.int32), zero_index])

    def device_tiles(device):
        start = (device * TILES_DEV).astype(jnp.int32)
        own = lax.dynamic_slice_in_dim(tiles, start, TILES_DEV, 0)
        own_rows = lax.dynamic_slice_in_dim(tile_rows, start, TILES_DEV, 0) % ROW_BLK
        own_cols = lax.dynamic_slice_in_dim(tile_cols, start, TILES_DEV, 0) % COL_BLK
        picked = table[device]
        return (own, own_rows, own_cols, padded[picked], mirror_rows[picked], mirror_cols[picked])

    def add_degree(degree_sum, device):
        own, own_rows, own_cols, taken, taken_rows, taken_cols = device_tiles(device)
        terms = jax.ops.segment_sum(jnp.sum(jnp.abs(own.astype(jnp.float32)), axis=2), own_rows, ROW_BLK)
        terms = terms + jax.ops.segment_sum(jnp.sum(jnp.abs(taken.astype(jnp.float32)), axis=1), taken_rows, ROW_BLK)
        begin = (device // N_COL * ROW_BLK).astype(jnp.int32)
        block = lax.dynamic_slice_in_dim(degree_sum, begin, ROW_BLK, 0)
        return (lax.dynamic_update_slice_in_dim(degree_sum, block + terms, begin, 0), None)
    device_list = jnp.arange(DEVICES, dtype=jnp.int32)
    degree_sum, unused = lax.scan(add_degree, jnp.zeros((BLOCKS, TILE), jnp.float32), device_list)
    degree = 1.0 + degree_sum.reshape(NODES, 1)
    current = embed
    final_output = embed.astype(jnp.float32)
    for iteration in range(ITERS):
        columns = column_order(current).astype(jnp.float32)

        def add_partial(summed, device, columns=columns):
            own, own_rows, own_cols, taken, taken_rows, taken_cols = device_tiles(device)
            begin = (device % N_COL * COL_ROWS).astype(jnp.int32)
            group = lax.dynamic_slice_in_dim(columns, begin, COL_ROWS, 0).reshape(COL_BLK, TILE, K)
            own_terms = jnp.einsum('nab,nbk->nak', own.astype(jnp.float32), group[own_cols], precision=lax.Precision.HIGHEST)
            taken_terms = jnp.einsum('nab,nak->nbk', taken.astype(jnp.float32), group[taken_cols], precision=lax.Precision.HIGHEST)
            partial_value = jax.ops.segment_sum(own_terms, own_rows, ROW_BLK) + jax.ops.segment_sum(taken_terms, taken_rows, ROW_BLK)
            rounded = lax.optimization_barrier(partial_value.astype(jnp.bfloat16)).astype(jnp.float32)
            row_begin = (device // N_COL * ROW_BLK).astype(jnp.int32)
            block = lax.dynamic_slice_in_dim(summed, row_begin, ROW_BLK, 0)
            return (lax.dynamic_update_slice_in_dim(summed, block + rounded, row_begin, 0), None)
        summed, unused = lax.scan(add_partial, jnp.zeros((BLOCKS, TILE, K), jnp.float32), device_list)
        scaled = summed.reshape(NODES, K) / degree
        gram = jnp.dot(scaled.T.astype(jnp.float32), scaled.astype(jnp.float32), precision=lax.Precision.HIGHEST, preferred_element_type=jnp.float32) / NODES
        lower = jnp.linalg.cholesky(gram)
        final_output = lax.linalg.triangular_solve(lower, scaled, left_side=False, lower=True, transpose_a=True)
        current = final_output.astype(jnp.bfloat16)
    return final_output
```

```python
import functools

import jax
import jax.numpy as jnp
from jax import lax
from jax.experimental import pallas as pl
from jax.experimental.pallas import tpu as pltpu
from jax.sharding import PartitionSpec as P

ITERS = 3
CAP = 3
F32 = jnp.float32
BF16 = jnp.bfloat16
VMEM = pl.BlockSpec(memory_space=pltpu.VMEM)
SMEM = pl.BlockSpec(memory_space=pltpu.SMEM)
ANY = pl.BlockSpec(memory_space=pl.ANY)
LIMIT = 32 * 1024 * 1024
BIG = 60 * 1024 * 1024


def exchange(value, axis, distance):
    size = lax.axis_size(axis)
    return lax.ppermute(value, axis, [(i, i ^ distance) for i in range(size)])


def pack_kernel(devices, row_blocks, col_blocks, col_count, rows, cols, chg, slots, places, counts, sem):
    total = slots.shape[0]

    def clear(i, carry):
        slots[i] = jnp.zeros(slots.shape[1:], slots.dtype)
        places[i] = 0
        return carry

    lax.fori_loop(0, total, clear, 0)

    def reset(i, carry):
        counts[i] = 0
        return carry

    lax.fori_loop(0, devices, reset, 0)

    def place(i, carry):
        row, col = cols[i], rows[i]
        owner = row // row_blocks * col_count + col // col_blocks
        rank = counts[owner]
        counts[owner] = rank + 1
        slot = owner * CAP + rank
        places[slot] = row % row_blocks * col_blocks + col % col_blocks
        pltpu.make_async_copy(chg.at[i], slots.at[slot], sem).start()
        return carry

    lax.fori_loop(0, chg.shape[0], place, 0)
    pltpu.make_async_copy(chg, slots.at[pl.ds(0, chg.shape[0])], sem).wait()


def degree_kernel(tile_rows, chg_cols, tiles, chg, tiles_t, degree):
    degree[...] = jnp.zeros(degree.shape, F32)

    def own(i, carry):
        tile = tiles[i].T
        tiles_t[i] = tile
        block = tile_rows[i]
        degree[pl.ds(block, 1), :] += jnp.sum(jnp.abs(tile.astype(F32)), axis=0, keepdims=True)
        return carry

    lax.fori_loop(0, tiles.shape[0], own, 0)

    def changed(i, carry):
        block = chg_cols[i]
        degree[pl.ds(block, 1), :] += jnp.sum(jnp.abs(chg[i].astype(F32)), axis=0, keepdims=True)
        return carry

    lax.fori_loop(0, chg.shape[0], changed, 0)


def merge_kernel(row_size, sub, place, *refs):
    outs = refs[-(refs[0].shape[1] // refs[-1].shape[2] // row_size) :]
    sources = refs[: len(refs) - len(outs)]
    features, tile = outs[0].shape[1:]
    groups = tile // sub
    member, family = place[0] % groups, place[0] // groups
    lane = lax.broadcasted_iota(jnp.int32, (features, tile), 1) // sub
    for distance, out in enumerate(outs):
        for r in range(row_size):
            block = r * len(outs) + jnp.bitwise_xor(family, distance)
            at = pl.ds(pl.multiple_of(block * tile, tile), tile)
            value = sources[0][:, at].astype(F32)
            for d in range(1, groups):
                g = jnp.bitwise_xor(member, d)
                moved = pltpu.roll(sources[d][:, at].astype(F32), (g - member) * sub % tile, 1)
                value = jnp.where(lane == g, moved, value)
            out[r] = value.astype(BF16)


def product_kernel(by_column, sub, row_size, core, own_rows, own_x, taken_rows, taken_x, tiles_t, taken, *rest):
    pieces, (keep, send), scratch = rest[:row_size], rest[row_size : row_size + 2], rest[row_size + 2 :]
    x_buf, own_buf, taken_buf, total, out_buf, x_sem, own_sem, taken_sem, out_sem = scratch
    per_device = pieces[0].shape[0]
    tile = own_buf.shape[1]
    x_copies = [
        pltpu.make_async_copy(piece, x_buf.at[pl.ds(i * per_device, per_device)], x_sem.at[i])
        for i, piece in enumerate(pieces)
    ]
    own_copy = pltpu.make_async_copy(tiles_t, own_buf, own_sem)
    taken_copy = pltpu.make_async_copy(taken, taken_buf, taken_sem)
    for copy in x_copies:
        copy.start()
    own_copy.start()
    taken_copy.start()

    def clear(i, carry):
        total[i] = jnp.zeros(total.shape[1:], F32)
        return carry

    lax.fori_loop(0, total.shape[0], clear, 0, unroll=8)
    for copy in x_copies:
        copy.wait()
    for copy, buf, rows, blocks in ((own_copy, own_buf, own_rows, own_x), (taken_copy, taken_buf, taken_rows, taken_x)):
        copy.wait()

        def add(i, carry, buf=buf, rows=rows, blocks=blocks):
            total[rows[i]] += jnp.dot(x_buf[blocks[i]], buf[i], preferred_element_type=F32)
            return carry

        lax.fori_loop(0, buf.shape[0], add, 0, unroll=8)
    half = out_buf.shape[1]
    groups = tile // sub
    if by_column:
        per_row = 2 * half // groups
        lane = lax.broadcasted_iota(jnp.int32, total.shape[1:], 1) // sub

        def regroup(r, carry):
            for part in range(per_row):
                for j in range(per_row):
                    base = j * groups * per_device + part + r * per_row
                    blocks = [total[base + g * per_device] for g in range(groups)]
                    for side in range(groups):
                        column = part * groups + side
                        value = blocks[0]
                        for g in range(groups):
                            shift = (g - side) * sub % tile
                            moved = pltpu.roll(blocks[g], shift, 1) if shift else blocks[g]
                            value = moved if g == 0 else jnp.where(lane == g, moved, value)
                        out_buf[column % 2, column // 2, r * per_row + j] = value.astype(BF16)
            return carry

        lax.fori_loop(0, row_size, regroup, 0)
    else:
        for chip in range(half):
            for side in range(2):

                def straight(i, carry, chip=chip, side=side):
                    out_buf[side, chip, i] = total[(2 * chip + side) * per_device + i].astype(BF16)
                    return carry

                lax.fori_loop(0, per_device, straight, 0, unroll=4)
    mine = core[0]
    keep_copy = pltpu.make_async_copy(out_buf.at[mine], keep, out_sem.at[0])
    send_copy = pltpu.make_async_copy(out_buf.at[1 - mine], send, out_sem.at[1])
    keep_copy.start()
    send_copy.start()
    keep_copy.wait()
    send_copy.wait()


def pair_kernel(chip, keep, other, *out):
    mine = chip[0]
    for i, piece in enumerate(out):
        there = jnp.bitwise_xor(mine, i + 1)

        def add(b, carry, piece=piece, there=there):
            piece[b] = (keep[there, b].astype(F32) + other[there, b].astype(F32)).astype(BF16)
            return carry

        lax.fori_loop(0, piece.shape[0], add, 0, unroll=4)


def scale_kernel(normalize, chip, keep, other, degree, inverse, *rest):
    received, (rounded, scaled) = rest[:-2], rest[-2:]
    mine = chip[0]

    def add(b, carry):
        total = keep[mine, b].astype(F32) + other[mine, b].astype(F32)
        for piece in received:
            total = total + piece[b].astype(F32)
        total = total / degree[pl.ds(b, 1), :]
        if normalize:
            total = jnp.dot(inverse[...], total, precision=lax.Precision.HIGHEST, preferred_element_type=F32)
        scaled[b] = total
        rounded[b] = total.astype(BF16)
        return carry

    lax.fori_loop(0, rounded.shape[0], add, 0, unroll=4)


def gram_kernel(scaled, gram):
    total = jnp.zeros(gram.shape, F32)
    for b in range(scaled.shape[0]):
        block = scaled[b]
        total = total + lax.dot_general(
            block, block, (((1,), (1,)), ((), ())), precision=lax.Precision.HIGHEST, preferred_element_type=F32
        )
    gram[...] = total


def final_kernel(scaled, inverse, out):
    tile = scaled.shape[2]
    for b in range(scaled.shape[0]):
        out[:, b * tile : (b + 1) * tile] = jnp.dot(
            inverse[...], scaled[b], precision=lax.Precision.HIGHEST, preferred_element_type=F32
        )


def params(limit=LIMIT):
    return pltpu.CompilerParams(vmem_limit_bytes=limit)


def sum_all(gram):
    for axis, distances in (("col", [1]), ("col", range(2, lax.axis_size("col"), 2)), ("row", range(1, lax.axis_size("row")))):
        parts = [exchange(gram, axis, d) for d in distances]
        for part in parts:
            gram = gram + part
    return gram


def inverse_factor(gram):
    lower = jnp.linalg.cholesky(gram)
    return lax.linalg.triangular_solve(lower, jnp.eye(gram.shape[0], dtype=F32), left_side=True, lower=True)


def local(embed, tiles, tile_rows, tile_cols, chg_tiles, chg_rows, chg_cols):
    rows_dev, features = embed.shape
    tile = tiles.shape[1]
    row_size, col_size = lax.axis_size("row"), lax.axis_size("col")
    devices = row_size * col_size
    per_device = rows_dev // tile
    row_blocks, col_blocks = per_device * col_size, per_device * row_size
    sub = rows_dev // devices
    groups = tile // sub
    per_row = col_size // groups
    half = col_size // 2
    nodes = rows_dev * devices
    row, col = lax.axis_index("row"), lax.axis_index("col")
    core = (col % 2).reshape(1)
    chip = (col // 2).reshape(1)
    block = jax.ShapeDtypeStruct((per_device, features, tile), BF16)
    block32 = jax.ShapeDtypeStruct((per_device, features, tile), F32)

    slots, places = pl.pallas_call(
        functools.partial(pack_kernel, devices, row_blocks, col_blocks, col_size),
        out_shape=(
            jax.ShapeDtypeStruct((devices * CAP, tile, tile), BF16),
            jax.ShapeDtypeStruct((devices * CAP,), jnp.int32),
        ),
        in_specs=[SMEM, SMEM, ANY],
        out_specs=(VMEM, SMEM),
        scratch_shapes=[pltpu.SMEM((devices,), jnp.int32), pltpu.SemaphoreType.DMA],
        compiler_params=params(),
        name="pack",
    )(chg_rows, chg_cols, chg_tiles)
    taken = lax.all_to_all(
        slots.reshape(devices, CAP, tile, tile), ("row", "col"), split_axis=0, concat_axis=0, tiled=True
    ).reshape(devices * CAP, tile, tile)
    embed, tiles, chg_tiles, places = lax.optimization_barrier((embed, tiles, chg_tiles, places))
    all_places = places[None]
    for axis, size in (("col", col_size), ("row", row_size)):
        distance = 1
        while distance < size:
            all_places = jnp.concatenate([all_places, exchange(all_places, axis, distance)], axis=0)
            distance *= 2
    me = row * col_size + col
    my_places = lax.dynamic_slice_in_dim(all_places, me * CAP, CAP, 1)
    my_places = my_places[jnp.bitwise_xor(jnp.arange(devices), me)].reshape(devices * CAP)

    def x_block(position, first):
        from_row = jnp.bitwise_xor(position % per_device // per_row, row) * per_device
        outer, inner = position // per_device, position % per_row
        if first:
            return from_row + jnp.bitwise_xor(inner, col // groups) * row_size + outer
        return from_row + outer * per_row + inner

    own_rows, own_cols = tile_rows % row_blocks, tile_cols % col_blocks
    taken_rows, taken_cols = my_places // col_blocks, my_places % col_blocks

    tiles_t, degree_terms = pl.pallas_call(
        degree_kernel,
        out_shape=(
            jax.ShapeDtypeStruct(tiles.shape, BF16),
            jax.ShapeDtypeStruct((row_blocks * row_size, tile), F32),
        ),
        in_specs=[SMEM, SMEM, VMEM, VMEM],
        out_specs=(VMEM, VMEM),
        compiler_params=params(),
        name="degree",
    )(tile_rows, chg_cols, tiles, chg_tiles)
    degree_terms = degree_terms.reshape(row_size, row_blocks, tile)
    degree = lax.dynamic_index_in_dim(degree_terms, row, 0, False)
    for d in range(1, row_size):
        degree = degree + exchange(
            lax.dynamic_index_in_dim(degree_terms, jnp.bitwise_xor(row, d), 0, False), "row", d
        )
    degree = degree + exchange(degree, "col", 1)
    degree = 1.0 + degree + sum(exchange(degree, "col", d) for d in range(2, col_size, 2))
    node_degree = lax.dynamic_slice_in_dim(degree, col * per_device, per_device, 0)
    column_degree = lax.dynamic_index_in_dim(
        degree.reshape(per_row, groups, row_size, col_size, sub), col, 3, False
    )
    column_degree = column_degree.transpose(2, 0, 1, 3).reshape(per_device, tile)

    embed_t = embed.T
    joined = pl.pallas_call(
        functools.partial(merge_kernel, row_size, sub),
        out_shape=(jax.ShapeDtypeStruct((row_size, features, tile), BF16),) * per_row,
        in_specs=[SMEM] + [VMEM] * groups,
        out_specs=(VMEM,) * per_row,
        compiler_params=params(),
        name="merge",
    )(col.reshape(1), embed_t, *[exchange(embed_t, "col", d) for d in range(1, groups)])
    current = jnp.concatenate(
        [joined[0]] + [exchange(joined[d], "col", d * groups) for d in range(1, per_row)], axis=0
    )
    inverse = jnp.eye(features, dtype=F32)
    scaled = None
    total_gram = None
    for iteration in range(ITERS):
        last = iteration == ITERS - 1
        gathered = [current] + [exchange(current, "row", d) for d in range(1, row_size)]
        if iteration:
            total_gram = sum_all(gram)
            gathered[0], total_gram = lax.optimization_barrier((gathered[0], total_gram))
        keep, send = pl.pallas_call(
            functools.partial(product_kernel, not last, sub, row_size),
            out_shape=(jax.ShapeDtypeStruct((half, *block.shape), BF16),) * 2,
            in_specs=[SMEM] * 5 + [ANY] * (2 + row_size),
            out_specs=(ANY, ANY),
            scratch_shapes=[
                pltpu.VMEM((row_size * per_device, features, tile), BF16),
                pltpu.VMEM(tiles.shape, BF16),
                pltpu.VMEM((devices * CAP, tile, tile), BF16),
                pltpu.VMEM((row_blocks, features, tile), F32),
                pltpu.VMEM((2, half, *block.shape), BF16),
                pltpu.SemaphoreType.DMA((row_size,)),
                pltpu.SemaphoreType.DMA,
                pltpu.SemaphoreType.DMA,
                pltpu.SemaphoreType.DMA((2,)),
            ],
            compiler_params=params(BIG),
            name="product",
        )(
            core, own_rows, x_block(own_cols, iteration == 0), taken_rows, x_block(taken_cols, iteration == 0),
            tiles_t, taken, *gathered,
        )
        other = exchange(send, "col", 1)
        paired = pl.pallas_call(
            pair_kernel,
            out_shape=(block,) * (half - 1),
            in_specs=[SMEM, VMEM, VMEM],
            out_specs=(VMEM,) * (half - 1),
            compiler_params=params(),
            name="pair",
        )(chip, keep, other)
        received = [exchange(piece, "col", 2 * (i + 1)) for i, piece in enumerate(paired)]
        if iteration:
            total_gram = lax.optimization_barrier((total_gram, paired[-1]))[0]
            inverse = inverse_factor(total_gram / nodes)
        current, scaled = pl.pallas_call(
            functools.partial(scale_kernel, iteration > 0),
            out_shape=(block, block32),
            in_specs=[SMEM] + [VMEM] * (4 + half - 1),
            out_specs=(VMEM, VMEM),
            compiler_params=params(),
            name="scale",
        )(chip, keep, other, node_degree if last else column_degree, inverse, *received)
        gram = pl.pallas_call(
            gram_kernel,
            out_shape=jax.ShapeDtypeStruct((features, features), F32),
            in_specs=[VMEM],
            out_specs=VMEM,
            compiler_params=params(),
            name="gram",
        )(scaled)
    inverse = inverse_factor(sum_all(gram) / nodes)
    out = pl.pallas_call(
        final_kernel,
        out_shape=jax.ShapeDtypeStruct((features, rows_dev), F32),
        in_specs=[VMEM, VMEM],
        out_specs=VMEM,
        compiler_params=params(),
        name="final",
    )(scaled, inverse)
    return out.T


def solution(mesh):
    placed = (
        P(("row", "col"), None),
        P(("row", "col"), None, None),
        P(("row", "col")),
        P(("row", "col")),
        P(("row", "col"), None, None),
        P(("row", "col")),
        P(("row", "col")),
    )
    return jax.shard_map(
        local, mesh=mesh, in_specs=placed, out_specs=P(("row", "col"), None), check_vma=False
    )
```

```python
import functools

import jax
import jax.numpy as jnp
from jax import lax
from jax.experimental import pallas as pl
from jax.experimental.pallas import tpu as pltpu
from jax.sharding import PartitionSpec as P

ITERS = 3
CAP = 3
F32 = jnp.float32
BF16 = jnp.bfloat16
VMEM = pl.BlockSpec(memory_space=pltpu.VMEM)
SMEM = pl.BlockSpec(memory_space=pltpu.SMEM)
ANY = pl.BlockSpec(memory_space=pl.ANY)
LIMIT = 32 * 1024 * 1024
BIG = 60 * 1024 * 1024
NONE = pl.CostEstimate(flops=0, bytes_accessed=0, transcendentals=0)


def exchange(value, axis, distance):
    size = lax.axis_size(axis)
    return lax.ppermute(value, axis, [(i, i ^ distance) for i in range(size)])


def pack_kernel(devices, row_blocks, col_blocks, col_count, rows_in, cols_in, chg, slots, places, rows, cols, counts, sems):
    listed = chg.shape[0]
    loads = [pltpu.make_async_copy(rows_in, rows, sems.at[0]), pltpu.make_async_copy(cols_in, cols, sems.at[1])]
    for load in loads:
        load.start()

    def clear(i, carry):
        slots[i] = jnp.zeros(slots.shape[1:], slots.dtype)
        return carry

    lax.fori_loop(0, slots.shape[0], clear, 0, unroll=4)

    def reset(i, carry):
        counts[i] = 0
        for k in range(CAP):
            places[i * CAP + k] = 0
        return carry

    lax.fori_loop(0, devices, reset, 0, unroll=4)
    for load in loads:
        load.wait()

    def place(i, carry):
        row, col = cols[i], rows[i]
        owner = lax.div(row, row_blocks) * col_count + lax.div(col, col_blocks)
        rank = counts[owner]
        counts[owner] = rank + 1
        slot = owner * CAP + rank
        places[slot] = lax.rem(row, row_blocks) * col_blocks + lax.rem(col, col_blocks)
        pltpu.make_async_copy(chg.at[i], slots.at[slot], sems.at[2]).start()
        return carry

    lax.fori_loop(0, listed, place, 0, unroll=4)

    pltpu.make_async_copy(chg, slots.at[pl.ds(0, listed)], sems.at[2]).wait()


def degree_kernel(tile_rows, tiles, tiles_t, degree):
    degree[...] = jnp.zeros(degree.shape, F32)

    def own(i, carry):
        tile = tiles[i].T
        tiles_t[i] = tile
        degree[pl.ds(tile_rows[i], 1), :] += jnp.sum(jnp.abs(tile.astype(F32)), axis=0, keepdims=True)
        return carry

    lax.fori_loop(0, tiles.shape[0], own, 0, unroll=4)


def two_parts(value):
    high = value.astype(BF16)
    return high, (value - high.astype(F32)).astype(BF16)


def one_part(block, at, rows):
    return block[at : at + rows].astype(F32) + block[at + rows : at + 2 * rows].astype(F32)


def merge_kernel(row_size, sub, place, notes, *refs):
    outs = refs[-(refs[0].shape[1] // refs[-1].shape[2] // row_size) :]
    sources = refs[: len(refs) - len(outs)]
    features, tile = outs[0].shape[1:]
    groups = tile // sub
    member, family = place[0] % groups, place[0] // groups
    lane = lax.broadcasted_iota(jnp.int32, (features, tile), 1) // sub
    for distance, out in enumerate(outs):
        for r in range(row_size):
            block = r * len(outs) + jnp.bitwise_xor(family, distance)
            at = pl.ds(pl.multiple_of(block * tile, tile), tile)
            value = sources[0][:, at].astype(F32)
            for d in range(1, groups):
                g = jnp.bitwise_xor(member, d)
                moved = pltpu.roll(sources[d][:, at].astype(F32), (g - member) * sub % tile, 1)
                value = jnp.where(lane == g, moved, value)
            out[r] = value.astype(BF16)
        out[row_size] = jnp.zeros(out.shape[1:], BF16)
        out[row_size, : notes.shape[1], :] = notes[distance]


def product_kernel(by_column, first, sub, per_device, row_size, held, core, own_rows, own_x, taken_rows, taken_x, *rest):
    if first:
        own_degree, rest = rest[0], rest[1:]
    tiles_t, taken, rest = rest[0], rest[1], rest[2:]
    pieces, (keep, send), scratch = rest[:held], rest[held : held + 2], rest[held + 2 :]
    x_buf, own_buf, taken_buf, total, out_buf, degree, part_buf, x_sem, own_sem, taken_sem, out_sem = scratch
    tile = own_buf.shape[1]
    x_copies = [
        pltpu.make_async_copy(piece.at[pl.ds(0, per_device)], x_buf.at[pl.ds(i * per_device, per_device)], x_sem.at[i])
        for i, piece in enumerate(pieces)
    ]
    own_copy = pltpu.make_async_copy(tiles_t, own_buf, own_sem)
    taken_copy = pltpu.make_async_copy(taken, taken_buf, taken_sem)
    for copy in x_copies:
        copy.start()
    own_copy.start()
    taken_copy.start()

    def clear(i, carry):
        total[i] = jnp.zeros(total.shape[1:], F32)
        return carry

    lax.fori_loop(0, total.shape[0], clear, 0, unroll=8)
    if first:
        degree[...] = own_degree[...]
    for copy in x_copies:
        copy.wait()
    for copy, buf, rows, blocks in ((own_copy, own_buf, own_rows, own_x), (taken_copy, taken_buf, taken_rows, taken_x)):
        copy.wait()

        def add(i, carry, buf=buf, rows=rows, blocks=blocks):
            total[rows[i]] += jnp.dot(x_buf[blocks[i]], buf[i], preferred_element_type=F32)
            if first and buf is taken_buf:
                degree[pl.ds(rows[i], 1), :] += jnp.sum(jnp.abs(buf[i].astype(F32)), axis=0, keepdims=True)
            return carry

        lax.fori_loop(0, buf.shape[0], add, 0, unroll=8)
    half = out_buf.shape[1]
    groups = tile // sub
    if by_column:
        per_row = 2 * half // groups
        lane = lax.broadcasted_iota(jnp.int32, total.shape[1:], 1) // sub

        def regroup(r, carry):
            for part in range(per_row):
                for j in range(per_row):
                    base = j * groups * per_device + part + r * per_row
                    blocks = [total[base + g * per_device] for g in range(groups)]
                    for side in range(groups):
                        column = part * groups + side
                        value = blocks[0]
                        for g in range(groups):
                            shift = (g - side) * sub % tile
                            moved = pltpu.roll(blocks[g], shift, 1) if shift else blocks[g]
                            value = moved if g == 0 else jnp.where(lane == g, moved, value)
                        out_buf[column % 2, column // 2, r * per_row + j] = value.astype(BF16)
            return carry

        lax.fori_loop(0, row_size, regroup, 0)
    else:
        for chip in range(half):
            for side in range(2):

                def straight(i, carry, chip=chip, side=side):
                    out_buf[side, chip, i] = total[(2 * chip + side) * per_device + i].astype(BF16)
                    return carry

                lax.fori_loop(0, per_device, straight, 0, unroll=4)
    if first:
        per_row = 2 * half // groups
        lane = lax.broadcasted_iota(jnp.int32, (row_size, tile), 1) // sub
        for column in range(2 * half):
            part, side = column // groups, column % groups
            for j in range(per_row):
                value = None
                for g in range(groups):
                    block = degree[pl.ds((j * groups + g) * per_device + part, row_size, stride=per_row), :]
                    shift = (g - side) * sub % tile
                    moved = pltpu.roll(block, shift, 1) if shift else block
                    value = moved if g == 0 else jnp.where(lane == g, moved, value)
                part_buf[pl.ds(j, row_size, stride=per_row), :] = value
            by_node = degree[column * per_device : (column + 1) * per_device, :]
            values = two_parts(part_buf[...]) + two_parts(by_node)
            out_buf[column % 2, column // 2, per_device] = jnp.concatenate(values, axis=0)
    mine = core[0]
    keep_copy = pltpu.make_async_copy(out_buf.at[mine], keep, out_sem.at[0])
    send_copy = pltpu.make_async_copy(out_buf.at[1 - mine], send, out_sem.at[1])
    keep_copy.start()
    send_copy.start()
    keep_copy.wait()
    send_copy.wait()


def pair_kernel(per_device, chip, keep, other, *out):
    mine = chip[0]
    for i, piece in enumerate(out):
        there = jnp.bitwise_xor(mine, i + 1)

        def add(b, carry, piece=piece, there=there):
            piece[b] = (keep[there, b].astype(F32) + other[there, b].astype(F32)).astype(BF16)
            return carry

        lax.fori_loop(0, per_device, add, 0, unroll=4)
        if piece.shape[0] > per_device:
            here, sent = keep[there, per_device], other[there, per_device]
            values = []
            for at in (0, 2 * per_device):
                values += two_parts(one_part(here, at, per_device) + one_part(sent, at, per_device))
            piece[per_device] = jnp.concatenate(values, axis=0)


def scale_kernel(normalize, last, first, chip, keep, other, *rest):
    mine = chip[0]
    if first:
        received, (out, scaled, degrees) = rest[:-3], rest[-3:]
        per_device = out.shape[0]
        parts = [keep[mine, per_device], other[mine, per_device]] + [piece[per_device] for piece in received]
        for i in range(2):
            degrees[i] = 1.0 + sum(one_part(part, 2 * i * per_device, per_device) for part in parts)
        degree = degrees.at[0]
        gram = jnp.zeros((1, 1), F32)
    else:
        degrees, inverse, rest = rest[0], rest[1], rest[2:]
        received, (out, scaled) = rest[:-2], rest[-2:]
        degree = degrees.at[1 if last else 0]
        gram = jnp.zeros(inverse.shape, F32)

    def add(b, gram):
        total = keep[mine, b].astype(F32) + other[mine, b].astype(F32)
        for piece in received:
            total = total + piece[b].astype(F32)
        total = total / degree[pl.ds(b, 1), :]
        if normalize:
            total = jnp.dot(inverse[...], total, precision=lax.Precision.HIGHEST, preferred_element_type=F32)
        scaled[b] = total
        if last:
            return gram + lax.dot_general(
                total, total, (((1,), (1,)), ((), ())), precision=lax.Precision.HIGHEST, preferred_element_type=F32
            )
        out[b] = total.astype(BF16)
        return gram

    gram = lax.fori_loop(0, scaled.shape[0], add, gram, unroll=4)
    if last:
        out[...] = gram


def gram_kernel(scaled, gram):
    total = jnp.zeros(gram.shape, F32)
    for b in range(scaled.shape[0]):
        block = scaled[b]
        total = total + lax.dot_general(
            block, block, (((1,), (1,)), ((), ())), precision=lax.Precision.HIGHEST, preferred_element_type=F32
        )
    gram[...] = total


def inverse_factor(gram):
    size, step = gram.shape[0], 8
    row = lax.broadcasted_iota(jnp.int32, (size, size), 0)
    lane = lax.broadcasted_iota(jnp.int32, (size, size), 1)
    both = jnp.concatenate([gram, (row == lane).astype(F32)], axis=1)
    rows = [both[i : i + step] for i in range(0, size, step)]
    within = lax.broadcasted_iota(jnp.int32, rows[0].shape, 0)
    for p in range(len(rows)):
        cols = {
            i: [jnp.broadcast_to(rows[i][:, p * step + k : p * step + k + 1], rows[i].shape) for k in range(step)]
            for i in range(p, len(rows))
        }
        for k in range(step):
            pivot = [cols[p][l][k : k + 1] for l in range(step)]
            pivot_row = rows[p][k : k + 1]
            one = 1.0 / pivot[k]
            for i in range(p, len(rows)):
                scale = cols[i][k] * one
                if i == p:
                    scale = jnp.where(within > k, scale, 0.0)
                for l in range(k + 1, step):
                    cols[i][l] = cols[i][l] - scale * pivot[l]
                rows[i] = rows[i] - scale * pivot_row
    both = jnp.concatenate(rows, axis=0)
    pivots = jnp.sum(jnp.where(row == lane, both[:, :size], 0.0), axis=1, keepdims=True)
    return both[:, size:] * lax.rsqrt(pivots)


def factor_kernel(nodes, *refs):
    grams, inverse = refs[:-1], refs[-1]
    inverse[...] = inverse_factor(sum(g[...] for g in grams) / nodes)


def final_kernel(nodes, scaled, *refs):
    grams, out = refs[:-1], refs[-1]
    inverse = inverse_factor(sum(g[...] for g in grams) / nodes)
    tile = scaled.shape[2]
    for b in range(scaled.shape[0]):
        out[:, b * tile : (b + 1) * tile] = jnp.dot(
            inverse, scaled[b], precision=lax.Precision.HIGHEST, preferred_element_type=F32
        )


def params(limit=LIMIT):
    return pltpu.CompilerParams(vmem_limit_bytes=limit)


def plane_parts(gram):
    gram = gram + exchange(gram, "col", 1)
    return [gram] + [exchange(gram, "col", d) for d in range(2, lax.axis_size("col"), 2)]


def along_row(gram):
    return [gram] + [exchange(gram, "row", d) for d in range(1, lax.axis_size("row"))]


def after(value, *marks):
    return lax.optimization_barrier((value, *marks))[0]


def local(embed, tiles, tile_rows, tile_cols, chg_tiles, chg_rows, chg_cols):
    rows_dev, features = embed.shape
    tile = tiles.shape[1]
    row_size, col_size = lax.axis_size("row"), lax.axis_size("col")
    devices = row_size * col_size
    per_device = rows_dev // tile
    row_blocks, col_blocks = per_device * col_size, per_device * row_size
    sub = rows_dev // devices
    groups = tile // sub
    per_row = col_size // groups
    half = col_size // 2
    note_rows = -(-groups * row_size * CAP * 2 // (16 * tile)) * 16
    nodes = rows_dev * devices
    row, col = lax.axis_index("row"), lax.axis_index("col")
    core = (col % 2).reshape(1)
    chip = (col // 2).reshape(1)
    block = jax.ShapeDtypeStruct((per_device, features, tile), BF16)
    block32 = jax.ShapeDtypeStruct((per_device, features, tile), F32)

    slots, places = pl.pallas_call(
        functools.partial(pack_kernel, devices, row_blocks, col_blocks, col_size),
        out_shape=(
            jax.ShapeDtypeStruct((devices * CAP, tile, tile), BF16),
            jax.ShapeDtypeStruct((devices * CAP,), jnp.int32),
        ),
        in_specs=[ANY, ANY, ANY],
        out_specs=(VMEM, SMEM),
        scratch_shapes=[
            pltpu.SMEM(chg_rows.shape, jnp.int32),
            pltpu.SMEM(chg_rows.shape, jnp.int32),
            pltpu.SMEM((devices,), jnp.int32),
            pltpu.SemaphoreType.DMA((3,)),
        ],
        compiler_params=params(BIG),
        cost_estimate=NONE,
        name="pack",
    )(chg_rows, chg_cols, chg_tiles)
    member, family = col % groups, col // groups
    group_places = jnp.stack([places] + [exchange(places, "col", d) for d in range(1, groups)])
    group_places = group_places.reshape(groups, row_size, col_size, CAP)
    notes = []
    for d in range(per_row):
        there = lax.dynamic_index_in_dim(group_places, jnp.bitwise_xor(family, d) * groups + member, 2, False)
        there = jnp.stack([there // col_blocks, there % col_blocks], axis=-1).reshape(-1)
        notes.append(jnp.pad(there, (0, note_rows * tile - there.size)).reshape(note_rows, tile))
    notes = jnp.stack(notes).astype(BF16)
    embed_t = embed.T
    joined = pl.pallas_call(
        functools.partial(merge_kernel, row_size, sub),
        out_shape=(jax.ShapeDtypeStruct((row_size + 1, features, tile), BF16),) * per_row,
        in_specs=[SMEM] + [VMEM] * (1 + groups),
        out_specs=(VMEM,) * per_row,
        compiler_params=params(),
        cost_estimate=NONE,
        name="merge",
    )(col.reshape(1), notes, embed_t, *[exchange(embed_t, "col", d) for d in range(1, groups)])
    joined = [joined[0]] + [exchange(joined[d], "col", d * groups) for d in range(1, per_row)]
    notes = jnp.concatenate([piece[row_size, :note_rows] for piece in joined], axis=0)
    notes = jnp.pad(notes, ((0, -notes.shape[0] % features), (0, 0))).reshape(-1, features, tile)
    current = jnp.concatenate([piece[:row_size] for piece in joined] + [notes], axis=0)
    steps = [(current, current)]
    for d in range(1, row_size):
        left, right = steps[-1]
        steps.append((
            lax.ppermute(left, "row", [(i, i + 1) for i in range(row_size - 1)]),
            lax.ppermute(right, "row", [(i + 1, i) for i in range(row_size - 1)]),
        ))
    gathered = [current] + [piece for pair in steps[1:] for piece in pair]

    def slot_of(source):
        away = jnp.abs(source - row)
        return jnp.where(away == 0, 0, 2 * away - 1 + (source > row))

    taken = lax.all_to_all(
        slots.reshape(devices, CAP, tile, tile), ("row", "col"), split_axis=0, concat_axis=0, tiled=True
    ).reshape(devices * CAP, tile, tile)
    notes = jnp.stack([piece[per_device:] for piece in gathered])[slot_of(jnp.arange(row_size))]
    notes = notes.reshape(row_size, -1, tile)[:, : per_row * note_rows].reshape(row_size, per_row, note_rows * tile)
    notes = notes[:, :, : groups * row_size * CAP * 2].reshape(row_size, per_row, groups, row_size, CAP, 2)
    notes = lax.dynamic_index_in_dim(notes, row, 3, False).reshape(row_size, col_size, CAP, 2)
    notes = notes[:, jnp.bitwise_xor(jnp.arange(col_size), col)].reshape(devices * CAP, 2).astype(jnp.int32)

    def x_block(position, first):
        source = position % per_device // per_row
        outer, inner = position // per_device, position % per_row
        if first:
            return slot_of(source) * per_device + jnp.bitwise_xor(inner, family) * row_size + outer
        return jnp.bitwise_xor(source, row) * per_device + outer * per_row + inner

    own_rows, own_cols = tile_rows % row_blocks, tile_cols % col_blocks
    taken_rows, taken_cols = notes[:, 0], notes[:, 1]

    tiles_t, own_degree = pl.pallas_call(
        degree_kernel,
        out_shape=(
            jax.ShapeDtypeStruct(tiles.shape, BF16),
            jax.ShapeDtypeStruct((row_blocks, tile), F32),
        ),
        in_specs=[SMEM, VMEM],
        out_specs=(VMEM, VMEM),
        compiler_params=params(),
        cost_estimate=NONE,
        name="degree",
    )(after(own_rows, joined[0]), tiles)
    for iteration in range(ITERS):
        first, last = iteration == 0, iteration == ITERS - 1
        blocks = per_device + 1 if first else per_device
        shape = (blocks, features, tile)
        if iteration:
            gathered = [current] + [exchange(current, "row", d) for d in range(1, row_size)]
        keep, send = pl.pallas_call(
            functools.partial(product_kernel, not last, first, sub, per_device, row_size, len(gathered)),
            out_shape=(jax.ShapeDtypeStruct((half, *shape), BF16),) * 2,
            in_specs=[SMEM] * 5 + [VMEM] * first + [ANY] * (2 + len(gathered)),
            out_specs=(ANY, ANY),
            scratch_shapes=[
                pltpu.VMEM((len(gathered) * per_device, features, tile), BF16),
                pltpu.VMEM(tiles.shape, BF16),
                pltpu.VMEM((devices * CAP, tile, tile), BF16),
                pltpu.VMEM((row_blocks, features, tile), F32),
                pltpu.VMEM((2, half, *shape), BF16),
                pltpu.VMEM((row_blocks, tile), F32),
                pltpu.VMEM((per_device, tile), F32),
                pltpu.SemaphoreType.DMA((len(gathered),)),
                pltpu.SemaphoreType.DMA,
                pltpu.SemaphoreType.DMA,
                pltpu.SemaphoreType.DMA((2,)),
            ],
            compiler_params=params(BIG),
            cost_estimate=NONE,
            name="product",
        )(
            core, own_rows, x_block(own_cols, iteration == 0), taken_rows, x_block(taken_cols, iteration == 0),
            *([own_degree] if first else []), tiles_t, taken, *gathered,
        )
        other = exchange(send, "col", 1)
        if iteration:
            gram = pl.pallas_call(
                gram_kernel,
                out_shape=jax.ShapeDtypeStruct((features, features), F32),
                in_specs=[VMEM],
                out_specs=VMEM,
                compiler_params=params(),
                cost_estimate=NONE,
                name="gram",
            )(after(scaled, keep))
            grams = along_row(sum(plane_parts(gram)))
        paired = pl.pallas_call(
            functools.partial(pair_kernel, per_device),
            out_shape=(jax.ShapeDtypeStruct(shape, BF16),) * (half - 1),
            in_specs=[SMEM, VMEM, VMEM],
            out_specs=(VMEM,) * (half - 1),
            compiler_params=params(),
            cost_estimate=NONE,
            name="pair",
        )(chip, keep, other)
        received = [exchange(piece, "col", 2 * (i + 1)) for i, piece in enumerate(paired)]
        if iteration:
            inverse = pl.pallas_call(
                functools.partial(factor_kernel, nodes),
                out_shape=jax.ShapeDtypeStruct((features, features), F32),
                in_specs=[VMEM] * len(grams),
                out_specs=VMEM,
                compiler_params=params(),
                cost_estimate=NONE,
                name="factor",
            )(*grams)
        square = jax.ShapeDtypeStruct((features, features), F32)
        both = jax.ShapeDtypeStruct((2, per_device, tile), F32)
        current, scaled, *found = pl.pallas_call(
            functools.partial(scale_kernel, not first, last, first),
            out_shape=(square if last else block, block32) + ((both,) if first else ()),
            in_specs=[SMEM] + [VMEM] * ((2 if first else 4) + half - 1),
            out_specs=(VMEM,) * (3 if first else 2),
            compiler_params=params(),
            cost_estimate=NONE,
            name="scale",
        )(chip, keep, other, *([] if first else [degrees, inverse]), *received)
        if first:
            degrees = found[0]
    out = pl.pallas_call(
        functools.partial(final_kernel, nodes),
        out_shape=jax.ShapeDtypeStruct((features, rows_dev), F32),
        in_specs=[VMEM] * (1 + row_size),
        out_specs=VMEM,
        compiler_params=params(),
        cost_estimate=NONE,
        name="final",
    )(scaled, *along_row(sum(plane_parts(current))))
    return out.T


def solution(mesh):
    placed = (
        P(("row", "col"), None),
        P(("row", "col"), None, None),
        P(("row", "col")),
        P(("row", "col")),
        P(("row", "col"), None, None),
        P(("row", "col")),
        P(("row", "col")),
    )
    return jax.shard_map(
        local, mesh=mesh, in_specs=placed, out_specs=P(("row", "col"), None), check_vma=False
    )
```

```python
import functools

import jax
import jax.numpy as jnp
from jax import lax
from jax.experimental import pallas as pl
from jax.experimental.pallas import tpu as pltpu
from jax.sharding import PartitionSpec as P

ITERS = 3
CAP = 3
F32 = jnp.float32
BF16 = jnp.bfloat16
VMEM = pl.BlockSpec(memory_space=pltpu.VMEM)
SMEM = pl.BlockSpec(memory_space=pltpu.SMEM)
ANY = pl.BlockSpec(memory_space=pl.ANY)
MIB = 1024 * 1024
LIMIT = 12 * MIB
BIG = 60 * MIB
NONE = pl.CostEstimate(flops=0, bytes_accessed=0, transcendentals=0)


def exchange(value, axis, distance):
    size = lax.axis_size(axis)
    return lax.ppermute(value, axis, [(i, i ^ distance) for i in range(size)])


def pack_kernel(devices, row_blocks, col_blocks, col_count, rows_in, cols_in, chg, slots, rows, cols, places, counts, sems):
    listed, tile = chg.shape[:2]
    loads = [pltpu.make_async_copy(rows_in, rows, sems.at[0]), pltpu.make_async_copy(cols_in, cols, sems.at[1])]
    for load in loads:
        load.start()

    def clear(i, carry):
        slots[i] = jnp.zeros(slots.shape[1:], slots.dtype)
        counts[i] = 0
        for k in range(2 * CAP):
            places[2 * CAP * i + k] = 0
        return carry

    lax.fori_loop(0, devices, clear, 0)
    for load in loads:
        load.wait()

    def place(i, carry):
        row, col = cols[i], rows[i]
        owner = lax.div(row, row_blocks) * col_count + lax.div(col, col_blocks)
        rank = counts[owner]
        counts[owner] = rank + 1
        at = 2 * (owner * CAP + rank)
        places[at] = lax.rem(row, row_blocks)
        places[at + 1] = lax.rem(col, col_blocks)
        there = pl.ds(pl.multiple_of(rank * tile, tile), tile)
        pltpu.make_async_copy(chg.at[i], slots.at[owner, there], sems.at[2]).start()
        return carry

    lax.fori_loop(0, listed, place, 0, unroll=4)
    pltpu.make_async_copy(chg, chg, sems.at[2]).wait()
    lane = lax.broadcasted_iota(jnp.int32, (16, tile), 1)

    def note(i, carry):
        value = jnp.zeros(lane.shape, jnp.int32)
        for k in range(2 * CAP):
            value = jnp.where(lane == k, places[2 * CAP * i + k], value)
        slots[i, CAP * tile :] = value.astype(F32).astype(BF16)
        return carry

    lax.fori_loop(0, devices, note, 0, unroll=2)


def stock_kernel(tile_rows, tiles, *refs):
    pieces, (stock, degree) = refs[:-2], refs[-2:]
    tile, count = tiles.shape[1], tiles.shape[0]
    features = stock.shape[1]
    per_tile = tile // features
    degree[...] = jnp.zeros(degree.shape, F32)

    def own(i, carry):
        value = tiles[i].T
        for k in range(per_tile):
            stock[i * per_tile + k] = value[k * features : (k + 1) * features]
        degree[pl.ds(tile_rows[i], 1), :] += jnp.sum(jnp.abs(value.astype(F32)), axis=0, keepdims=True)
        return carry

    lax.fori_loop(0, count, own, 0, unroll=4)
    at = count * per_tile
    for piece in pieces:
        stock[at : at + piece.shape[0]] = piece[...]
        at += piece.shape[0]
    high, low = two_parts(degree[...])
    for part in (high, low):
        for k in range(0, part.shape[0], features):
            stock[at] = part[k : k + features]
            at += 1


def two_parts(value):
    high = value.astype(BF16)
    return high, (value - high.astype(F32)).astype(BF16)


def one_part(block, at, rows):
    return block[at : at + rows].astype(F32) + block[at + rows : at + 2 * rows].astype(F32)


def merge_kernel(row_size, sub, place, *refs):
    features, tile = refs[-1].shape[1:]
    groups = tile // sub
    sources, outs = refs[: row_size * groups], refs[row_size * groups :]
    member, family = place[0] % groups, place[0] // groups
    lane = lax.broadcasted_iota(jnp.int32, (features, tile), 1) // sub
    for distance, out in enumerate(outs):
        for source in range(row_size):

            def join(r, carry, distance=distance, out=out, source=source):
                block = r * len(outs) + jnp.bitwise_xor(family, distance)
                at = pl.ds(pl.multiple_of(block * tile, tile), tile)
                value = sources[source * groups][:, at].astype(F32)
                for d in range(1, groups):
                    g = jnp.bitwise_xor(member, d)
                    moved = pltpu.roll(sources[source * groups + d][:, at].astype(F32), (g - member) * sub % tile, 1)
                    value = jnp.where(lane == g, moved, value)
                out[source * row_size + r] = value.astype(BF16)
                return carry

            lax.fori_loop(0, row_size, join, 0, unroll=4)


def product_kernel(by_column, first, sub, per_device, row_size, chips, held, place, own_rows, own_x, *rest):
    if not first:
        numbers, grams, rest = rest[0], rest[1 : 1 + chips], rest[1 + chips :]
    stock, taken, rest = rest[0], rest[1], rest[2:]
    pieces, outs, found, scratch = rest[:held], rest[held : held + 2], rest[held + 2], rest[held + 3 :]
    x_buf, total, degree, part_buf = scratch[:4]
    half, (features, tile) = outs[0].shape[0], stock.shape[1:]
    per_tile = tile // features
    tile_count = own_rows.shape[0]
    groups = tile // sub
    per_row = 2 * half // groups
    total[...] = jnp.zeros(total.shape, F32)
    if first:
        number_buf, numbers, sems = scratch[4:]
        x_start, x_blocks = tile_count * per_tile, per_device * row_size
        parts, rows = stock.shape[0] - (x_start + x_blocks), degree.shape[0]
        own_degree = stock[x_start + x_blocks :].reshape(parts * features, tile).astype(F32)
        degree[...] = own_degree[:rows] + own_degree[rows:]
        note = taken[:, CAP * tile :].astype(F32)[:, 0, :].astype(jnp.int32)
        lane = lax.broadcasted_iota(jnp.int32, note.shape, 1)
        per_row_bits, per_device_bits = per_row.bit_length() - 1, per_device.bit_length() - 1
        inner, outer = jnp.bitwise_and(note, per_row - 1), jnp.right_shift(note, per_device_bits)
        source = jnp.bitwise_xor(jnp.right_shift(jnp.bitwise_and(note, per_device - 1), per_row_bits), place[2])
        block = (jnp.bitwise_xor(inner, place[1]) * row_size + source) * row_size + outer
        even = jnp.bitwise_and(lane, 1) == 0
        number_buf[...] = jnp.where(even, note, block)
        found[...] = jnp.where(even, note, source * per_device + outer * per_row + inner)
        numbers_copy = pltpu.make_async_copy(number_buf, numbers, sems)
        numbers_copy.start()
    else:
        found[...] = sum(gram[...] for gram in grams)
        for i, piece in enumerate(pieces):
            x_buf[i * per_device : (i + 1) * per_device] = piece[...]

    def x_block(block):
        return stock[x_start + block] if first else x_buf[block]

    def add_own(i, carry):
        value = stock[pl.ds(i * per_tile, per_tile)].reshape(tile, tile)
        total[own_rows[i]] += jnp.dot(x_block(own_x[i]), value, preferred_element_type=F32)
        return carry

    lax.fori_loop(0, tile_count, add_own, 0, unroll=8)
    if first:
        numbers_copy.wait()

    def add_taken(i, carry):
        for k in range(CAP):
            row, block = numbers[i, 2 * k], numbers[i, 2 * k + 1]
            value = taken[i, k * tile : (k + 1) * tile]
            if first:
                degree[pl.ds(row, 1), :] += jnp.sum(jnp.abs(value.astype(F32)), axis=0, keepdims=True)
            total[row] += jnp.dot(x_block(block), value, preferred_element_type=F32)
        return carry

    lax.fori_loop(0, taken.shape[0], add_taken, 0, unroll=4)

    def write(mine):
        lane = lax.broadcasted_iota(jnp.int32, total.shape[1:], 1) // sub

        def regroup(r, carry):
            for part in range(per_row):
                for j in range(per_row):
                    base = j * groups * per_device + part + r * per_row
                    blocks = [total[base + g * per_device] for g in range(groups)]
                    for side in range(groups):
                        column = part * groups + side
                        value = blocks[0]
                        for g in range(groups):
                            shift = (g - side) * sub % tile
                            moved = pltpu.roll(blocks[g], shift, 1) if shift else blocks[g]
                            value = moved if g == 0 else jnp.where(lane == g, moved, value)
                        outs[(column + mine) % 2][column // 2, r * per_row + j] = value.astype(BF16)
            return carry

        def straight(i, carry):
            for column in range(2 * half):
                outs[(column + mine) % 2][column // 2, i] = total[column * per_device + i].astype(BF16)
            return carry

        if by_column:
            lax.fori_loop(0, row_size, regroup, 0)
        else:
            lax.fori_loop(0, per_device, straight, 0)
        if not first:
            return
        lane = lax.broadcasted_iota(jnp.int32, (row_size, tile), 1) // sub
        for column in range(2 * half):
            part, side = column // groups, column % groups
            for j in range(per_row):
                value = None
                for g in range(groups):
                    block = degree[pl.ds((j * groups + g) * per_device + part, row_size, stride=per_row), :]
                    shift = (g - side) * sub % tile
                    moved = pltpu.roll(block, shift, 1) if shift else block
                    value = moved if g == 0 else jnp.where(lane == g, moved, value)
                part_buf[pl.ds(j, row_size, stride=per_row), :] = value
            by_node = degree[column * per_device : (column + 1) * per_device, :]
            values = two_parts(part_buf[...]) + two_parts(by_node)
            outs[(column + mine) % 2][column // 2, per_device] = jnp.concatenate(values, axis=0)

    for mine in range(2):
        pl.when(place[0] == mine)(functools.partial(write, mine))


def pair_kernel(per_device, chip, keep, other, *out):
    for i, piece in enumerate(out):
        there = jnp.bitwise_xor(chip[0], (i + 1) % len(out))

        def add(b, carry, piece=piece, there=there):
            piece[b] = (keep[there, b].astype(F32) + other[there, b].astype(F32)).astype(piece.dtype)
            return carry

        lax.fori_loop(0, per_device, add, 0, unroll=4)
        if piece.shape[0] > per_device:
            here, sent = keep[there, per_device], other[there, per_device]
            for at in (0, 2 * per_device):
                value = one_part(here, at, per_device) + one_part(sent, at, per_device)
                high, low = two_parts(value)
                piece[per_device, at : at + per_device] = high.astype(piece.dtype)
                piece[per_device, at + per_device : at + 2 * per_device] = low.astype(piece.dtype)


def scale_kernel(normalize, last, first, own, *rest):
    if first:
        received, (out, scaled, degrees) = rest[:-3], rest[-3:]
        per_device = out.shape[0]
        parts = [own[per_device]] + [piece[per_device] for piece in received]
        for i in range(2):
            degrees[i] = 1.0 + sum(one_part(part, 2 * i * per_device, per_device) for part in parts)
        degree = degrees.at[0]
        gram = jnp.zeros((1, 1), F32)
    else:
        degrees, inverse, rest = rest[0], rest[1], rest[2:]
        received, (out, scaled) = rest[:-2], rest[-2:]
        degree = degrees.at[1 if last else 0]
        gram = jnp.zeros(inverse.shape, F32)

    def add(b, gram):
        total = own[b]
        for piece in received:
            total = total + piece[b].astype(F32)
        total = total / degree[pl.ds(b, 1), :]
        if normalize:
            total = jnp.dot(inverse[...], total, precision=lax.Precision.HIGHEST, preferred_element_type=F32)
        scaled[b] = total
        if last:
            return gram + lax.dot_general(
                total, total, (((1,), (1,)), ((), ())), precision=lax.Precision.HIGHEST, preferred_element_type=F32
            )
        out[b] = total.astype(BF16)
        return gram

    gram = lax.fori_loop(0, scaled.shape[0], add, gram, unroll=scaled.shape[0] if last else 4)
    if last:
        out[...] = gram


def gram_kernel(scaled, mark, gram):
    total = jnp.zeros(gram.shape, F32)
    for b in range(scaled.shape[0]):
        block = scaled[b]
        total = total + lax.dot_general(
            block, block, (((1,), (1,)), ((), ())), precision=lax.Precision.HIGHEST, preferred_element_type=F32
        )
    gram[...] = total


def inverse_factor(gram):
    size, step = gram.shape[0], 8
    row = lax.broadcasted_iota(jnp.int32, (size, size), 0)
    lane = lax.broadcasted_iota(jnp.int32, (size, size), 1)
    both = jnp.concatenate([gram, (row == lane).astype(F32)], axis=1)
    rows = [both[i : i + step] for i in range(0, size, step)]
    within = lax.broadcasted_iota(jnp.int32, rows[0].shape, 0)
    for p in range(len(rows)):
        cols = {
            i: [jnp.broadcast_to(rows[i][:, p * step + k : p * step + k + 1], rows[i].shape) for k in range(step)]
            for i in range(p, len(rows))
        }
        for k in range(step):
            pivot = [cols[p][l][k : k + 1] for l in range(step)]
            pivot_row = rows[p][k : k + 1]
            one = 1.0 / pivot[k]
            for i in range(p, len(rows)):
                scale = cols[i][k] * one
                if i == p:
                    scale = jnp.where(within > k, scale, 0.0)
                for l in range(k + 1, step):
                    cols[i][l] = cols[i][l] - scale * pivot[l]
                rows[i] = rows[i] - scale * pivot_row
    both = jnp.concatenate(rows, axis=0)
    pivots = jnp.sum(jnp.where(row == lane, both[:, :size], 0.0), axis=1, keepdims=True)
    return both[:, size:] * lax.rsqrt(pivots)


def factor_kernel(nodes, *refs):
    grams, inverse = refs[:-1], refs[-1]
    inverse[...] = inverse_factor(sum(g[...] for g in grams) / nodes)


def final_kernel(nodes, scaled, *refs):
    grams, out = refs[:-1], refs[-1]
    inverse = inverse_factor(sum(g[...] for g in grams) / nodes)
    tile = scaled.shape[2]
    for b in range(scaled.shape[0]):
        out[:, b * tile : (b + 1) * tile] = jnp.dot(
            inverse, scaled[b], precision=lax.Precision.HIGHEST, preferred_element_type=F32
        )


def params(limit=LIMIT):
    return pltpu.CompilerParams(vmem_limit_bytes=limit)


def chip_parts(gram):
    return [gram] + [exchange(gram, "col", d) for d in range(2, lax.axis_size("col"), 2)]


def along_row(gram):
    return [gram] + [exchange(gram, "row", d) for d in range(1, lax.axis_size("row"))]


def local(embed, tiles, tile_rows, tile_cols, chg_tiles, chg_rows, chg_cols):
    rows_dev, features = embed.shape
    tile = tiles.shape[1]
    row_size, col_size = lax.axis_size("row"), lax.axis_size("col")
    devices = row_size * col_size
    per_device = rows_dev // tile
    row_blocks, col_blocks = per_device * col_size, per_device * row_size
    sub = rows_dev // devices
    groups = tile // sub
    per_row = col_size // groups
    half = col_size // 2
    product_limit = 2 * (tiles.size + 3 * devices * CAP * tile * tile // 2 + 8 * row_blocks * features * tile) + 6 * MIB
    nodes = rows_dev * devices
    row, col = lax.axis_index("row"), lax.axis_index("col")
    chip = (col // 2).reshape(1)
    block = jax.ShapeDtypeStruct((per_device, features, tile), BF16)
    block32 = jax.ShapeDtypeStruct((per_device, features, tile), F32)

    member, family = col % groups, col // groups
    embed_t = embed.T
    raw = [embed_t] + [exchange(embed_t, "row", d) for d in range(1, row_size)]
    slots = pl.pallas_call(
        functools.partial(pack_kernel, devices, row_blocks, col_blocks, col_size),
        out_shape=jax.ShapeDtypeStruct((devices, CAP * tile + 16, tile), BF16),
        in_specs=[ANY, ANY, ANY],
        out_specs=VMEM,
        scratch_shapes=[
            pltpu.SMEM(chg_rows.shape, jnp.int32),
            pltpu.SMEM(chg_rows.shape, jnp.int32),
            pltpu.SMEM((devices * CAP * 2,), jnp.int32),
            pltpu.SMEM((devices,), jnp.int32),
            pltpu.SemaphoreType.DMA((3,)),
        ],
        compiler_params=params(BIG),
        cost_estimate=NONE,
        name="pack",
    )(chg_rows, chg_cols, chg_tiles)
    gathered = pl.pallas_call(
        functools.partial(merge_kernel, row_size, sub),
        out_shape=(jax.ShapeDtypeStruct((row_size * row_size, features, tile), BF16),) * per_row,
        in_specs=[SMEM] + [VMEM] * (row_size * groups),
        out_specs=(VMEM,) * per_row,
        compiler_params=params(2 * rows_dev * features * row_size * (groups + row_size) + 8 * MIB),
        cost_estimate=NONE,
        name="merge",
    )(
        col.reshape(1),
        *[piece if d == 0 else exchange(piece, "col", d) for piece in raw for d in range(groups)],
    )
    gathered = [gathered[0]] + [exchange(gathered[d], "col", d * groups) for d in range(1, per_row)]
    slots = lax.optimization_barrier((slots, *raw[1:]))[0]
    taken = lax.all_to_all(slots, ("row", "col"), split_axis=0, concat_axis=0, tiled=True)

    def x_block(position, first):
        source = position % per_device // per_row
        outer, inner = position // per_device, position % per_row
        if first:
            return (jnp.bitwise_xor(inner, family) * row_size + jnp.bitwise_xor(source, row)) * row_size + outer
        return jnp.bitwise_xor(source, row) * per_device + outer * per_row + inner

    own_rows, own_cols = tile_rows % row_blocks, tile_cols % col_blocks
    per_tile = tile // features
    stock_blocks = tiles.shape[0] * per_tile + col_blocks + 2 * row_blocks // features
    stock = pl.pallas_call(
        stock_kernel,
        out_shape=jax.ShapeDtypeStruct((stock_blocks, features, tile), BF16),
        in_specs=[SMEM] + [VMEM] * (1 + len(gathered)),
        out_specs=VMEM,
        scratch_shapes=[pltpu.VMEM((row_blocks, tile), F32)],
        compiler_params=params(4 * tiles.size + 4 * stock_blocks * features * tile + 4 * MIB),
        cost_estimate=NONE,
        name="stock",
    )(own_rows, tiles, *gathered)

    place = jnp.stack([col % 2, family, row])
    square = jax.ShapeDtypeStruct((features, features), F32)
    numbers_shape = jax.ShapeDtypeStruct((devices, tile), jnp.int32)
    for iteration in range(ITERS):
        first, last = iteration == 0, iteration == ITERS - 1
        blocks = per_device + 1 if first else per_device
        shape = (blocks, features, tile)
        if iteration:
            gathered = [current] + [exchange(current, "row", d) for d in range(1, row_size)]
            gram = pl.pallas_call(
                gram_kernel,
                out_shape=jax.ShapeDtypeStruct((features, features), F32),
                in_specs=[VMEM, VMEM],
                out_specs=VMEM,
                compiler_params=params(),
                cost_estimate=NONE,
                name="gram",
            )(scaled, gathered[1])
            grams = chip_parts(gram + exchange(gram, "col", 1))
        keep, send, found = pl.pallas_call(
            functools.partial(product_kernel, not last, first, sub, per_device, row_size, half, 0 if first else len(gathered)),
            out_shape=(jax.ShapeDtypeStruct((half, *shape), BF16),) * 2 + (numbers_shape if first else square,),
            in_specs=[SMEM] * 3 + ([VMEM] * 2 if first else [SMEM] + [VMEM] * (2 + half + row_size)),
            out_specs=(VMEM, VMEM, VMEM),
            scratch_shapes=[
                pltpu.VMEM((1 if first else col_blocks, features, tile), BF16),
                pltpu.VMEM((row_blocks, features, tile), F32),
                pltpu.VMEM((row_blocks, tile), F32),
                pltpu.VMEM((per_device, tile), F32),
            ] + first * [
                pltpu.VMEM((devices, tile), jnp.int32),
                pltpu.SMEM((devices, tile), jnp.int32),
                pltpu.SemaphoreType.DMA,
            ],
            compiler_params=params(product_limit),
            cost_estimate=NONE,
            name="product",
        )(
            place, own_rows, x_block(own_cols, first),
            *([] if first else [numbers, *grams]), stock, taken, *([] if first else gathered),
        )
        other = exchange(send, "col", 1)
        if iteration:
            grams = along_row(found)
        else:
            numbers = found
        paired = pl.pallas_call(
            functools.partial(pair_kernel, per_device),
            out_shape=(jax.ShapeDtypeStruct(shape, BF16),) * (half - 1) + (jax.ShapeDtypeStruct(shape, F32),),
            in_specs=[SMEM, VMEM, VMEM],
            out_specs=(VMEM,) * half,
            compiler_params=params(),
            cost_estimate=NONE,
            name="pair",
        )(chip, keep, other)
        received = [exchange(piece, "col", 2 * (i + 1)) for i, piece in enumerate(paired[:-1])]
        if iteration:
            inverse = pl.pallas_call(
                functools.partial(factor_kernel, nodes),
                out_shape=jax.ShapeDtypeStruct((features, features), F32),
                in_specs=[VMEM] * len(grams),
                out_specs=VMEM,
                compiler_params=params(),
                cost_estimate=NONE,
                name="factor",
            )(*grams)
        both = jax.ShapeDtypeStruct((2, per_device, tile), F32)
        current, scaled, *rest = pl.pallas_call(
            functools.partial(scale_kernel, not first, last, first),
            out_shape=(square if last else block, block32) + ((both,) if first else ()),
            in_specs=[VMEM] * ((1 if first else 3) + half - 1),
            out_specs=(VMEM,) * (3 if first else 2),
            compiler_params=params(),
            cost_estimate=NONE,
            name="scale",
        )(paired[-1], *([] if first else [degrees, inverse]), *received)
        if first:
            degrees = rest[0]
    out = pl.pallas_call(
        functools.partial(final_kernel, nodes),
        out_shape=jax.ShapeDtypeStruct((features, rows_dev), F32),
        in_specs=[VMEM] * (1 + row_size),
        out_specs=VMEM,
        compiler_params=params(),
        cost_estimate=NONE,
        name="final",
    )(scaled, *along_row(sum(chip_parts(current + exchange(current, "col", 1)))))
    return out.T


def solution(mesh):
    placed = (
        P(("row", "col"), None),
        P(("row", "col"), None, None),
        P(("row", "col")),
        P(("row", "col")),
        P(("row", "col"), None, None),
        P(("row", "col")),
        P(("row", "col")),
    )
    return jax.shard_map(
        local, mesh=mesh, in_specs=placed, out_specs=P(("row", "col"), None), check_vma=False
    )
```

```python
import functools

import jax
import jax.numpy as jnp
from jax import lax
from jax.experimental import pallas as pl
from jax.experimental.pallas import tpu as pltpu
from jax.sharding import PartitionSpec as P

ITERS = 3
CAP = 3
PARTS = 2
F32 = jnp.float32
BF16 = jnp.bfloat16
VMEM = pl.BlockSpec(memory_space=pltpu.VMEM)
SMEM = pl.BlockSpec(memory_space=pltpu.SMEM)
ANY = pl.BlockSpec(memory_space=pl.ANY)
MIB = 1024 * 1024
LIMIT = 12 * MIB
BIG = 60 * MIB
NONE = pl.CostEstimate(flops=0, bytes_accessed=0, transcendentals=0)


def exchange(value, axis, distance):
    size = lax.axis_size(axis)
    return lax.ppermute(value, axis, [(i, i ^ distance) for i in range(size)])


def pack_kernel(devices, row_blocks, col_blocks, col_count, rows_in, cols_in, chg, slots, rows, cols, places, counts, sems):
    listed, tile = chg.shape[:2]
    loads = [pltpu.make_async_copy(rows_in, rows, sems.at[0]), pltpu.make_async_copy(cols_in, cols, sems.at[1])]
    for load in loads:
        load.start()

    def clear(i, carry):
        slots[i] = jnp.zeros(slots.shape[1:], slots.dtype)
        counts[i] = 0
        for k in range(2 * CAP):
            places[2 * CAP * i + k] = 0
        return carry

    lax.fori_loop(0, devices, clear, 0)
    for load in loads:
        load.wait()

    def place(i, carry):
        row, col = cols[i], rows[i]
        owner = lax.div(row, row_blocks) * col_count + lax.div(col, col_blocks)
        rank = counts[owner]
        counts[owner] = rank + 1
        at = 2 * (owner * CAP + rank)
        places[at] = lax.rem(row, row_blocks)
        places[at + 1] = lax.rem(col, col_blocks)
        there = pl.ds(pl.multiple_of(rank * tile, tile), tile)
        pltpu.make_async_copy(chg.at[i], slots.at[owner, there], sems.at[2]).start()
        return carry

    lax.fori_loop(0, listed, place, 0, unroll=4)
    pltpu.make_async_copy(chg, chg, sems.at[2]).wait()
    lane = lax.broadcasted_iota(jnp.int32, (16, tile), 1)

    def note(i, carry):
        value = jnp.zeros(lane.shape, jnp.int32)
        for k in range(2 * CAP):
            value = jnp.where(lane == k, places[2 * CAP * i + k], value)
        slots[i, CAP * tile :] = value.astype(F32).astype(BF16)
        return carry

    lax.fori_loop(0, devices, note, 0, unroll=2)


def stock_kernel(early, row_size, tile_rows, tiles, *refs):
    pieces, (stock, degree) = refs[:-2], refs[-2:]
    tile, count = tiles.shape[1], tiles.shape[0]
    features = stock.shape[1]
    per_tile = tile // features
    degree[...] = jnp.zeros(degree.shape, F32)

    def own(i, carry):
        value = tiles[i].T
        for k in range(per_tile):
            stock[i * per_tile + k] = value[k * features : (k + 1) * features]
        degree[pl.ds(tile_rows[i], 1), :] += jnp.sum(jnp.abs(value.astype(F32)), axis=0, keepdims=True)
        return carry

    lax.fori_loop(0, count, own, 0, unroll=4)
    at = count * per_tile
    families = len(pieces) - (row_size - len(early))
    late = list(pieces[families:])
    for d in range(row_size):
        if d in early:
            start = early.index(d) * row_size
            for family in range(families):
                stock[at : at + row_size] = pieces[family][start : start + row_size]
                at += row_size
        else:
            piece = late.pop(0)
            stock[at : at + piece.shape[0]] = piece[...]
            at += piece.shape[0]
    high, low = two_parts(degree[...])
    for part in (high, low):
        for k in range(0, part.shape[0], features):
            stock[at] = part[k : k + features]
            at += 1


def two_parts(value):
    high = value.astype(BF16)
    return high, (value - high.astype(F32)).astype(BF16)


def one_part(block, at, rows):
    return block[at : at + rows].astype(F32) + block[at + rows : at + 2 * rows].astype(F32)


def merge_kernel(count, row_size, sub, place, *refs):
    features, tile = refs[-1].shape[1:]
    groups = tile // sub
    sources, outs = refs[: count * groups], refs[count * groups :]
    member, family = place[0] % groups, place[0] // groups
    lane = lax.broadcasted_iota(jnp.int32, (features, tile), 1) // sub
    for distance, out in enumerate(outs):
        for source in range(count):

            def join(r, carry, distance=distance, out=out, source=source):
                block = r * len(outs) + jnp.bitwise_xor(family, distance)
                at = pl.ds(pl.multiple_of(block * tile, tile), tile)
                value = sources[source * groups][:, at].astype(F32)
                for d in range(1, groups):
                    g = jnp.bitwise_xor(member, d)
                    moved = pltpu.roll(sources[source * groups + d][:, at].astype(F32), (g - member) * sub % tile, 1)
                    value = jnp.where(lane == g, moved, value)
                out[source * row_size + r] = value.astype(BF16)
                return carry

            lax.fori_loop(0, row_size, join, 0, unroll=4)


def product_kernel(by_column, first, sub, per_device, row_size, chips, held, place, own_rows, own_x, *rest):
    if not first:
        numbers, grams, rest = rest[0], rest[1 : 1 + chips], rest[1 + chips :]
    stock, taken, rest = rest[0], rest[1], rest[2:]
    pieces, outs, found, scratch = rest[:held], rest[held : held + 2], rest[held + 2], rest[held + 3 :]
    x_buf, total, degree, part_buf = scratch[:4]
    half, (features, tile) = outs[0].shape[0], stock.shape[1:]
    per_tile = tile // features
    tile_count = own_rows.shape[0]
    groups = tile // sub
    per_row = 2 * half // groups
    total[...] = jnp.zeros(total.shape, F32)
    if first:
        number_buf, numbers, sems = scratch[4:]
        x_start, x_blocks = tile_count * per_tile, per_device * row_size
        parts, rows = stock.shape[0] - (x_start + x_blocks), degree.shape[0]
        own_degree = stock[x_start + x_blocks :].reshape(parts * features, tile).astype(F32)
        degree[...] = own_degree[:rows] + own_degree[rows:]
        note = taken[:, CAP * tile :].astype(F32)[:, 0, :].astype(jnp.int32)
        lane = lax.broadcasted_iota(jnp.int32, note.shape, 1)
        per_row_bits, per_device_bits = per_row.bit_length() - 1, per_device.bit_length() - 1
        inner, outer = jnp.bitwise_and(note, per_row - 1), jnp.right_shift(note, per_device_bits)
        source = jnp.bitwise_xor(jnp.right_shift(jnp.bitwise_and(note, per_device - 1), per_row_bits), place[2])
        block = (source * per_row + jnp.bitwise_xor(inner, place[1])) * row_size + outer
        even = jnp.bitwise_and(lane, 1) == 0
        number_buf[...] = jnp.where(even, note, block)
        found[...] = jnp.where(even, note, source * per_device + outer * per_row + inner)
        numbers_copy = pltpu.make_async_copy(number_buf, numbers, sems)
        numbers_copy.start()
    else:
        found[...] = sum(gram[...] for gram in grams)
        size = per_device // PARTS
        for i, piece in enumerate(pieces):
            x_buf[i * size : (i + 1) * size] = piece[...]

    def x_block(block):
        return stock[x_start + block] if first else x_buf[block]

    def add_own(i, carry):
        value = stock[pl.ds(i * per_tile, per_tile)].reshape(tile, tile)
        total[own_rows[i]] += jnp.dot(x_block(own_x[i]), value, preferred_element_type=F32)
        return carry

    lax.fori_loop(0, tile_count, add_own, 0, unroll=8)
    if first:
        numbers_copy.wait()

    def add_taken(i, carry):
        for k in range(CAP):
            row, block = numbers[i, 2 * k], numbers[i, 2 * k + 1]
            value = taken[i, k * tile : (k + 1) * tile]
            if first:
                degree[pl.ds(row, 1), :] += jnp.sum(jnp.abs(value.astype(F32)), axis=0, keepdims=True)
            total[row] += jnp.dot(x_block(block), value, preferred_element_type=F32)
        return carry

    lax.fori_loop(0, taken.shape[0], add_taken, 0, unroll=4)

    def write(mine):
        lane = lax.broadcasted_iota(jnp.int32, total.shape[1:], 1) // sub

        def regroup(r, carry):
            for part in range(per_row):
                for j in range(per_row):
                    base = j * groups * per_device + part + r * per_row
                    blocks = [total[base + g * per_device] for g in range(groups)]
                    for side in range(groups):
                        column = part * groups + side
                        value = blocks[0]
                        for g in range(groups):
                            shift = (g - side) * sub % tile
                            moved = pltpu.roll(blocks[g], shift, 1) if shift else blocks[g]
                            value = moved if g == 0 else jnp.where(lane == g, moved, value)
                        outs[(column + mine) % 2][column // 2, r * per_row + j] = value.astype(BF16)
            return carry

        def straight(i, carry):
            for column in range(2 * half):
                outs[(column + mine) % 2][column // 2, i] = total[column * per_device + i].astype(BF16)
            return carry

        if by_column:
            lax.fori_loop(0, row_size, regroup, 0)
        else:
            lax.fori_loop(0, per_device, straight, 0)
        if not first:
            return
        lane = lax.broadcasted_iota(jnp.int32, (row_size, tile), 1) // sub
        for column in range(2 * half):
            part, side = column // groups, column % groups
            for j in range(per_row):
                value = None
                for g in range(groups):
                    block = degree[pl.ds((j * groups + g) * per_device + part, row_size, stride=per_row), :]
                    shift = (g - side) * sub % tile
                    moved = pltpu.roll(block, shift, 1) if shift else block
                    value = moved if g == 0 else jnp.where(lane == g, moved, value)
                part_buf[pl.ds(j, row_size, stride=per_row), :] = value
            by_node = degree[column * per_device : (column + 1) * per_device, :]
            values = two_parts(part_buf[...]) + two_parts(by_node)
            outs[(column + mine) % 2][column // 2, per_device] = jnp.concatenate(values, axis=0)

    for mine in range(2):
        pl.when(place[0] == mine)(functools.partial(write, mine))


def pair_kernel(per_device, chip, keep, other, *out):
    for i, piece in enumerate(out):
        there = jnp.bitwise_xor(chip[0], (i + 1) % len(out))

        def add(b, carry, piece=piece, there=there):
            piece[b] = (keep[there, b].astype(F32) + other[there, b].astype(F32)).astype(piece.dtype)
            return carry

        lax.fori_loop(0, per_device, add, 0, unroll=4)
        if piece.shape[0] > per_device:
            here, sent = keep[there, per_device], other[there, per_device]
            for at in (0, 2 * per_device):
                value = one_part(here, at, per_device) + one_part(sent, at, per_device)
                high, low = two_parts(value)
                piece[per_device, at : at + per_device] = high.astype(piece.dtype)
                piece[per_device, at + per_device : at + 2 * per_device] = low.astype(piece.dtype)


def scale_kernel(normalize, last, first, own, *rest):
    if first:
        received, (*out, scaled, degrees) = rest[: -2 - PARTS], rest[-2 - PARTS :]
        per_device = scaled.shape[0]
        parts = [own[per_device]] + [piece[per_device] for piece in received]
        for i in range(2):
            degrees[i] = 1.0 + sum(one_part(part, 2 * i * per_device, per_device) for part in parts)
        degree = degrees.at[0]
        gram = jnp.zeros((1, 1), F32)
    else:
        degrees, inverse, rest = rest[0], rest[1], rest[2:]
        made = 1 if last else PARTS
        received, (*out, scaled) = rest[: -1 - made], rest[-1 - made :]
        degree = degrees.at[1 if last else 0]
        gram = jnp.zeros(inverse.shape, F32)

    size = scaled.shape[0] // PARTS

    def add(b, gram, part=0):
        total = own[b]
        for piece in received:
            total = total + piece[b].astype(F32)
        total = total / degree[pl.ds(b, 1), :]
        if normalize:
            total = jnp.dot(inverse[...], total, precision=lax.Precision.HIGHEST, preferred_element_type=F32)
        scaled[b] = total
        if last:
            return gram + lax.dot_general(
                total, total, (((1,), (1,)), ((), ())), precision=lax.Precision.HIGHEST, preferred_element_type=F32
            )
        out[part][b - part * size] = total.astype(BF16)
        return gram

    if last:
        out[0][...] = lax.fori_loop(0, scaled.shape[0], add, gram, unroll=scaled.shape[0])
        return
    for part in range(PARTS):
        lax.fori_loop(part * size, (part + 1) * size, functools.partial(add, part=part), gram, unroll=4)


def gram_kernel(scaled, mark, gram):
    total = jnp.zeros(gram.shape, F32)
    for b in range(scaled.shape[0]):
        block = scaled[b]
        total = total + lax.dot_general(
            block, block, (((1,), (1,)), ((), ())), precision=lax.Precision.HIGHEST, preferred_element_type=F32
        )
    gram[...] = total


def inverse_factor(gram):
    size, step = gram.shape[0], 8
    row = lax.broadcasted_iota(jnp.int32, (size, size), 0)
    lane = lax.broadcasted_iota(jnp.int32, (size, size), 1)
    both = jnp.concatenate([gram, (row == lane).astype(F32)], axis=1)
    rows = [both[i : i + step] for i in range(0, size, step)]
    within = lax.broadcasted_iota(jnp.int32, rows[0].shape, 0)
    for p in range(len(rows)):
        cols = {
            i: [jnp.broadcast_to(rows[i][:, p * step + k : p * step + k + 1], rows[i].shape) for k in range(step)]
            for i in range(p, len(rows))
        }
        for k in range(step):
            pivot = [cols[p][l][k : k + 1] for l in range(step)]
            pivot_row = rows[p][k : k + 1]
            one = 1.0 / pivot[k]
            for i in range(p, len(rows)):
                scale = cols[i][k] * one
                if i == p:
                    scale = jnp.where(within > k, scale, 0.0)
                for l in range(k + 1, step):
                    cols[i][l] = cols[i][l] - scale * pivot[l]
                rows[i] = rows[i] - scale * pivot_row
    both = jnp.concatenate(rows, axis=0)
    pivots = jnp.sum(jnp.where(row == lane, both[:, :size], 0.0), axis=1, keepdims=True)
    return both[:, size:] * lax.rsqrt(pivots)


def factor_kernel(nodes, *refs):
    grams, inverse = refs[:-1], refs[-1]
    inverse[...] = inverse_factor(sum(g[...] for g in grams) / nodes)


def final_kernel(nodes, scaled, *refs):
    grams, out = refs[:-1], refs[-1]
    inverse = inverse_factor(sum(g[...] for g in grams) / nodes)
    tile = scaled.shape[2]
    for b in range(scaled.shape[0]):
        out[:, b * tile : (b + 1) * tile] = jnp.dot(
            inverse, scaled[b], precision=lax.Precision.HIGHEST, preferred_element_type=F32
        )


def params(limit=LIMIT):
    return pltpu.CompilerParams(vmem_limit_bytes=limit)


def chip_parts(gram):
    return [gram] + [exchange(gram, "col", d) for d in range(2, lax.axis_size("col"), 2)]


def along_row(gram):
    return [gram] + [exchange(gram, "row", d) for d in range(1, lax.axis_size("row"))]


def local(embed, tiles, tile_rows, tile_cols, chg_tiles, chg_rows, chg_cols):
    rows_dev, features = embed.shape
    tile = tiles.shape[1]
    row_size, col_size = lax.axis_size("row"), lax.axis_size("col")
    devices = row_size * col_size
    per_device = rows_dev // tile
    row_blocks, col_blocks = per_device * col_size, per_device * row_size
    sub = rows_dev // devices
    groups = tile // sub
    per_row = col_size // groups
    half = col_size // 2
    product_limit = 2 * (tiles.size + 3 * devices * CAP * tile * tile // 2 + 8 * row_blocks * features * tile) + 6 * MIB
    nodes = rows_dev * devices
    row, col = lax.axis_index("row"), lax.axis_index("col")
    chip = (col // 2).reshape(1)
    block = jax.ShapeDtypeStruct((per_device, features, tile), BF16)
    block32 = jax.ShapeDtypeStruct((per_device, features, tile), F32)

    member, family = col % groups, col // groups
    embed_t = embed.T
    early = [d for d in range(row_size) if d & (d - 1) == 0]
    raw = [embed_t] + [exchange(embed_t, "row", d) for d in early[1:]]
    slots = pl.pallas_call(
        functools.partial(pack_kernel, devices, row_blocks, col_blocks, col_size),
        out_shape=jax.ShapeDtypeStruct((devices, CAP * tile + 16, tile), BF16),
        in_specs=[ANY, ANY, ANY],
        out_specs=VMEM,
        scratch_shapes=[
            pltpu.SMEM(chg_rows.shape, jnp.int32),
            pltpu.SMEM(chg_rows.shape, jnp.int32),
            pltpu.SMEM((devices * CAP * 2,), jnp.int32),
            pltpu.SMEM((devices,), jnp.int32),
            pltpu.SemaphoreType.DMA((3,)),
        ],
        compiler_params=params(BIG),
        cost_estimate=NONE,
        name="pack",
    )(chg_rows, chg_cols, chg_tiles)
    merged = pl.pallas_call(
        functools.partial(merge_kernel, len(early), row_size, sub),
        out_shape=(jax.ShapeDtypeStruct((len(early) * row_size, features, tile), BF16),) * per_row,
        in_specs=[SMEM] + [VMEM] * (len(early) * groups),
        out_specs=(VMEM,) * per_row,
        compiler_params=params(2 * rows_dev * features * len(early) * (groups + row_size) + 8 * MIB),
        cost_estimate=NONE,
        name="merge",
    )(
        col.reshape(1),
        *[piece if d == 0 else exchange(piece, "col", d) for piece in raw for d in range(groups)],
    )
    gathered = [merged[0]] + [exchange(merged[d], "col", d * groups) for d in range(1, per_row)]
    complete = {}
    for d in range(1, row_size):
        if d in early:
            at = early.index(d) * row_size
            complete[d] = jnp.concatenate([piece[at : at + row_size] for piece in gathered], axis=0)
        else:
            complete[d] = exchange(complete[d & (d - 1)], "row", d & -d)
    late = [complete[d] for d in range(row_size) if d not in early]
    slots = lax.optimization_barrier((slots, *raw[1:]))[0]
    taken = lax.all_to_all(slots, ("row", "col"), split_axis=0, concat_axis=0, tiled=True)

    def x_block(position, first):
        source = position % per_device // per_row
        outer, inner = position // per_device, position % per_row
        if first:
            return (jnp.bitwise_xor(source, row) * per_row + jnp.bitwise_xor(inner, family)) * row_size + outer
        return jnp.bitwise_xor(source, row) * per_device + outer * per_row + inner

    own_rows, own_cols = tile_rows % row_blocks, tile_cols % col_blocks
    per_tile = tile // features
    stock_blocks = tiles.shape[0] * per_tile + col_blocks + 2 * row_blocks // features
    stock = pl.pallas_call(
        functools.partial(stock_kernel, early, row_size),
        out_shape=jax.ShapeDtypeStruct((stock_blocks, features, tile), BF16),
        in_specs=[SMEM] + [VMEM] * (1 + len(gathered) + len(late)),
        out_specs=VMEM,
        scratch_shapes=[pltpu.VMEM((row_blocks, tile), F32)],
        compiler_params=params(4 * tiles.size + 4 * stock_blocks * features * tile + 4 * MIB),
        cost_estimate=NONE,
        name="stock",
    )(own_rows, tiles, *gathered, *late)

    place = jnp.stack([col % 2, family, row])
    square = jax.ShapeDtypeStruct((features, features), F32)
    numbers_shape = jax.ShapeDtypeStruct((devices, tile), jnp.int32)
    for iteration in range(ITERS):
        first, last = iteration == 0, iteration == ITERS - 1
        blocks = per_device + 1 if first else per_device
        shape = (blocks, features, tile)
        if iteration:
            gathered = {0: current}
            for d in sorted(range(1, row_size), key=lambda d: (d & (d - 1) != 0, -d if d & (d - 1) == 0 else d)):
                low = d & -d
                gathered[d] = [exchange(part, "row", low) for part in gathered[d ^ low]]
            first_part = gathered[row_size // 2][0]
            gathered = [part for d in range(row_size) for part in gathered[d]]
            gram = pl.pallas_call(
                gram_kernel,
                out_shape=jax.ShapeDtypeStruct((features, features), F32),
                in_specs=[VMEM, VMEM],
                out_specs=VMEM,
                compiler_params=params(),
                cost_estimate=NONE,
                name="gram",
            )(scaled, first_part)
            grams = chip_parts(gram + exchange(gram, "col", 1))
        keep, send, found = pl.pallas_call(
            functools.partial(product_kernel, not last, first, sub, per_device, row_size, half, 0 if first else len(gathered)),
            out_shape=(jax.ShapeDtypeStruct((half, *shape), BF16),) * 2 + (numbers_shape if first else square,),
            in_specs=[SMEM] * 3 + ([VMEM] * 2 if first else [SMEM] + [VMEM] * (2 + half + len(gathered))),
            out_specs=(VMEM, VMEM, VMEM),
            scratch_shapes=[
                pltpu.VMEM((1 if first else col_blocks, features, tile), BF16),
                pltpu.VMEM((row_blocks, features, tile), F32),
                pltpu.VMEM((row_blocks, tile), F32),
                pltpu.VMEM((per_device, tile), F32),
            ] + first * [
                pltpu.VMEM((devices, tile), jnp.int32),
                pltpu.SMEM((devices, tile), jnp.int32),
                pltpu.SemaphoreType.DMA,
            ],
            compiler_params=params(product_limit),
            cost_estimate=NONE,
            name="product",
        )(
            place, own_rows, x_block(own_cols, first),
            *([] if first else [numbers, *grams]), stock, taken, *([] if first else gathered),
        )
        other = exchange(send, "col", 1)
        if iteration:
            grams = along_row(found)
        else:
            numbers = found
        paired = pl.pallas_call(
            functools.partial(pair_kernel, per_device),
            out_shape=(jax.ShapeDtypeStruct(shape, BF16),) * (half - 1) + (jax.ShapeDtypeStruct(shape, F32),),
            in_specs=[SMEM, VMEM, VMEM],
            out_specs=(VMEM,) * half,
            compiler_params=params(),
            cost_estimate=NONE,
            name="pair",
        )(chip, keep, other)
        received = [exchange(piece, "col", 2 * (i + 1)) for i, piece in enumerate(paired[:-1])]
        if iteration:
            inverse = pl.pallas_call(
                functools.partial(factor_kernel, nodes),
                out_shape=jax.ShapeDtypeStruct((features, features), F32),
                in_specs=[VMEM] * len(grams),
                out_specs=VMEM,
                compiler_params=params(),
                cost_estimate=NONE,
                name="factor",
            )(*grams)
        both = jax.ShapeDtypeStruct((2, per_device, tile), F32)
        piece = jax.ShapeDtypeStruct((per_device // PARTS, features, tile), BF16)
        *current, scaled = pl.pallas_call(
            functools.partial(scale_kernel, not first, last, first),
            out_shape=((square,) if last else (piece,) * PARTS) + (block32,) + ((both,) if first else ()),
            in_specs=[VMEM] * ((1 if first else 3) + half - 1),
            out_specs=(VMEM,) * (2 if last else PARTS + 2 if first else PARTS + 1),
            compiler_params=params(),
            cost_estimate=NONE,
            name="scale",
        )(paired[-1], *([] if first else [degrees, inverse]), *received)
        if first:
            *current, scaled, degrees = *current, scaled
    out = pl.pallas_call(
        functools.partial(final_kernel, nodes),
        out_shape=jax.ShapeDtypeStruct((features, rows_dev), F32),
        in_specs=[VMEM] * (1 + row_size),
        out_specs=VMEM,
        compiler_params=params(),
        cost_estimate=NONE,
        name="final",
    )(scaled, *along_row(sum(chip_parts(current[0] + exchange(current[0], "col", 1)))))
    return out.T


def solution(mesh):
    placed = (
        P(("row", "col"), None),
        P(("row", "col"), None, None),
        P(("row", "col")),
        P(("row", "col")),
        P(("row", "col"), None, None),
        P(("row", "col")),
        P(("row", "col")),
    )
    return jax.shard_map(
        local, mesh=mesh, in_specs=placed, out_specs=P(("row", "col"), None), check_vma=False
    )
```

```python
import functools

import jax
import jax.numpy as jnp
from jax import lax
from jax.experimental import pallas as pl
from jax.experimental.pallas import tpu as pltpu
from jax.sharding import PartitionSpec as P

ITERS = 3
CAP = 3
PARTS = 2
F32 = jnp.float32
BF16 = jnp.bfloat16
VMEM = pl.BlockSpec(memory_space=pltpu.VMEM)
SMEM = pl.BlockSpec(memory_space=pltpu.SMEM)
ANY = pl.BlockSpec(memory_space=pl.ANY)
MIB = 1024 * 1024
LIMIT = 12 * MIB
BIG = 60 * MIB
NONE = pl.CostEstimate(flops=0, bytes_accessed=0, transcendentals=0)


def exchange(value, axis, distance):
    size = lax.axis_size(axis)
    return lax.ppermute(value, axis, [(i, i ^ distance) for i in range(size)])


def pack_kernel(devices, row_blocks, col_blocks, col_count, rows_in, cols_in, chg, slots, rows, cols, places, counts, sems):
    listed, tile = chg.shape[:2]
    loads = [pltpu.make_async_copy(rows_in, rows, sems.at[0]), pltpu.make_async_copy(cols_in, cols, sems.at[1])]
    for load in loads:
        load.start()

    def clear(i, carry):
        slots[i] = jnp.zeros(slots.shape[1:], slots.dtype)
        counts[i] = 0
        for k in range(2 * CAP):
            places[2 * CAP * i + k] = 0
        return carry

    lax.fori_loop(0, devices, clear, 0)
    for load in loads:
        load.wait()

    def place(i, carry):
        row, col = cols[i], rows[i]
        owner = lax.div(row, row_blocks) * col_count + lax.div(col, col_blocks)
        rank = counts[owner]
        counts[owner] = rank + 1
        at = 2 * (owner * CAP + rank)
        places[at] = lax.rem(row, row_blocks)
        places[at + 1] = lax.rem(col, col_blocks)
        there = pl.ds(pl.multiple_of(rank * tile, tile), tile)
        pltpu.make_async_copy(chg.at[i], slots.at[owner, there], sems.at[2]).start()
        return carry

    lax.fori_loop(0, listed, place, 0, unroll=4)
    pltpu.make_async_copy(chg, chg, sems.at[2]).wait()
    lane = lax.broadcasted_iota(jnp.int32, (16, tile), 1)

    def note(i, carry):
        value = jnp.zeros(lane.shape, jnp.int32)
        for k in range(2 * CAP):
            value = jnp.where(lane == k, places[2 * CAP * i + k], value)
        slots[i, CAP * tile :] = value.astype(F32).astype(BF16)
        return carry

    lax.fori_loop(0, devices, note, 0, unroll=2)


def stock_kernel(early, row_size, tile_rows, tiles, *refs):
    pieces, (stock, degree) = refs[:-2], refs[-2:]
    tile, count = tiles.shape[1], tiles.shape[0]
    features = stock.shape[1]
    per_tile = tile // features
    degree[...] = jnp.zeros(degree.shape, F32)

    def own(i, carry):
        value = tiles[i].T
        for k in range(per_tile):
            stock[i * per_tile + k] = value[k * features : (k + 1) * features]
        degree[pl.ds(tile_rows[i], 1), :] += jnp.sum(jnp.abs(value.astype(F32)), axis=0, keepdims=True)
        return carry

    lax.fori_loop(0, count, own, 0, unroll=4)
    at = count * per_tile
    families = len(pieces) - (row_size - len(early))
    late = list(pieces[families:])
    for d in range(row_size):
        if d in early:
            start = early.index(d) * row_size
            for family in range(families):
                stock[at : at + row_size] = pieces[family][start : start + row_size]
                at += row_size
        else:
            piece = late.pop(0)
            stock[at : at + piece.shape[0]] = piece[...]
            at += piece.shape[0]
    high, low = two_parts(degree[...])
    for part in (high, low):
        for k in range(0, part.shape[0], features):
            stock[at] = part[k : k + features]
            at += 1


def two_parts(value):
    high = value.astype(BF16)
    return high, (value - high.astype(F32)).astype(BF16)


def one_part(block, at, rows):
    return block[at : at + rows].astype(F32) + block[at + rows : at + 2 * rows].astype(F32)


def merge_kernel(count, row_size, sub, place, *refs):
    features, tile = refs[-1].shape[1:]
    groups = tile // sub
    sources, outs = refs[: count * groups], refs[count * groups :]
    member, family = place[0] % groups, place[0] // groups
    lane = lax.broadcasted_iota(jnp.int32, (features, tile), 1) // sub
    for distance, out in enumerate(outs):
        for source in range(count):

            def join(r, carry, distance=distance, out=out, source=source):
                block = r * len(outs) + jnp.bitwise_xor(family, distance)
                at = pl.ds(pl.multiple_of(block * tile, tile), tile)
                value = sources[source * groups][:, at].astype(F32)
                for d in range(1, groups):
                    g = jnp.bitwise_xor(member, d)
                    moved = pltpu.roll(sources[source * groups + d][:, at].astype(F32), (g - member) * sub % tile, 1)
                    value = jnp.where(lane == g, moved, value)
                out[source * row_size + r] = value.astype(BF16)
                return carry

            lax.fori_loop(0, row_size, join, 0, unroll=4)


def product_kernel(by_column, first, sub, per_device, row_size, chips, held, place, own_rows, own_x, *rest):
    if not first:
        numbers, grams, rest = rest[0], rest[1 : 1 + chips], rest[1 + chips :]
    stock, taken, rest = rest[0], rest[1], rest[2:]
    pieces, outs, found, scratch = rest[:held], rest[held : held + 2], rest[held + 2], rest[held + 3 :]
    x_buf, total, degree, part_buf = scratch[:4]
    half, (features, tile) = outs[0].shape[0], stock.shape[1:]
    per_tile = tile // features
    tile_count = own_rows.shape[0]
    groups = tile // sub
    per_row = 2 * half // groups
    total[...] = jnp.zeros(total.shape, F32)
    if first:
        number_buf, numbers, sems = scratch[4:]
        x_start, x_blocks = tile_count * per_tile, per_device * row_size
        parts, rows = stock.shape[0] - (x_start + x_blocks), degree.shape[0]
        own_degree = stock[x_start + x_blocks :].reshape(parts * features, tile).astype(F32)
        degree[...] = own_degree[:rows] + own_degree[rows:]
        note = taken[:, CAP * tile :].astype(F32)[:, 0, :].astype(jnp.int32)
        lane = lax.broadcasted_iota(jnp.int32, note.shape, 1)
        per_row_bits, per_device_bits = per_row.bit_length() - 1, per_device.bit_length() - 1
        inner, outer = jnp.bitwise_and(note, per_row - 1), jnp.right_shift(note, per_device_bits)
        source = jnp.bitwise_xor(jnp.right_shift(jnp.bitwise_and(note, per_device - 1), per_row_bits), place[2])
        block = (source * per_row + jnp.bitwise_xor(inner, place[1])) * row_size + outer
        even = jnp.bitwise_and(lane, 1) == 0
        number_buf[...] = jnp.where(even, note, block)
        found[...] = jnp.where(even, note, source * per_device + outer * per_row + inner)
        numbers_copy = pltpu.make_async_copy(number_buf, numbers, sems)
        numbers_copy.start()
    else:
        found[...] = sum(gram[...] for gram in grams)
        size = per_device // PARTS
        for i, piece in enumerate(pieces):
            x_buf[i * size : (i + 1) * size] = piece[...]

    def x_block(block):
        return stock[x_start + block] if first else x_buf[block]

    def add_own(i, carry):
        value = stock[pl.ds(i * per_tile, per_tile)].reshape(tile, tile)
        total[own_rows[i]] += jnp.dot(x_block(own_x[i]), value, preferred_element_type=F32)
        return carry

    lax.fori_loop(0, tile_count, add_own, 0, unroll=64)
    if first:
        numbers_copy.wait()

    def add_taken(i, carry):
        for k in range(CAP):
            row, block = numbers[i, 2 * k], numbers[i, 2 * k + 1]
            value = taken[i, k * tile : (k + 1) * tile]
            if first:
                degree[pl.ds(row, 1), :] += jnp.sum(jnp.abs(value.astype(F32)), axis=0, keepdims=True)
            total[row] += jnp.dot(x_block(block), value, preferred_element_type=F32)
        return carry

    lax.fori_loop(0, taken.shape[0], add_taken, 0, unroll=16 if first else 32)

    def write(mine):
        lane = lax.broadcasted_iota(jnp.int32, total.shape[1:], 1) // sub

        def regroup(r, carry):
            for part in range(per_row):
                for j in range(per_row):
                    base = j * groups * per_device + part + r * per_row
                    blocks = [total[base + g * per_device] for g in range(groups)]
                    for side in range(groups):
                        column = part * groups + side
                        value = blocks[0]
                        for g in range(groups):
                            shift = (g - side) * sub % tile
                            moved = pltpu.roll(blocks[g], shift, 1) if shift else blocks[g]
                            value = moved if g == 0 else jnp.where(lane == g, moved, value)
                        outs[(column + mine) % 2][column // 2, r * per_row + j] = value.astype(BF16)
            return carry

        def straight(i, carry):
            for column in range(2 * half):
                outs[(column + mine) % 2][column // 2, i] = total[column * per_device + i].astype(BF16)
            return carry

        if by_column:
            lax.fori_loop(0, row_size, regroup, 0, unroll=2)
        else:
            lax.fori_loop(0, per_device, straight, 0, unroll=4)
        if not first:
            return
        lane = lax.broadcasted_iota(jnp.int32, (row_size, tile), 1) // sub
        for column in range(2 * half):
            part, side = column // groups, column % groups
            for j in range(per_row):
                value = None
                for g in range(groups):
                    block = degree[pl.ds((j * groups + g) * per_device + part, row_size, stride=per_row), :]
                    shift = (g - side) * sub % tile
                    moved = pltpu.roll(block, shift, 1) if shift else block
                    value = moved if g == 0 else jnp.where(lane == g, moved, value)
                part_buf[pl.ds(j, row_size, stride=per_row), :] = value
            by_node = degree[column * per_device : (column + 1) * per_device, :]
            values = two_parts(part_buf[...]) + two_parts(by_node)
            outs[(column + mine) % 2][column // 2, per_device] = jnp.concatenate(values, axis=0)

    for mine in range(2):
        pl.when(place[0] == mine)(functools.partial(write, mine))


def pair_kernel(per_device, chip, keep, other, *out):
    for i, piece in enumerate(out):
        there = jnp.bitwise_xor(chip[0], (i + 1) % len(out))

        def add(b, carry, piece=piece, there=there):
            piece[b] = (keep[there, b].astype(F32) + other[there, b].astype(F32)).astype(piece.dtype)
            return carry

        lax.fori_loop(0, per_device, add, 0, unroll=4)
        if piece.shape[0] > per_device:
            here, sent = keep[there, per_device], other[there, per_device]
            for at in (0, 2 * per_device):
                value = one_part(here, at, per_device) + one_part(sent, at, per_device)
                high, low = two_parts(value)
                piece[per_device, at : at + per_device] = high.astype(piece.dtype)
                piece[per_device, at + per_device : at + 2 * per_device] = low.astype(piece.dtype)


def scale_kernel(normalize, last, first, own, *rest):
    if first:
        received, (*out, scaled, degrees) = rest[: -2 - PARTS], rest[-2 - PARTS :]
        per_device = scaled.shape[0]
        parts = [own[per_device]] + [piece[per_device] for piece in received]
        for i in range(2):
            degrees[i] = 1.0 + sum(one_part(part, 2 * i * per_device, per_device) for part in parts)
        degree = degrees.at[0]
    else:
        degrees, inverse, rest = rest[0], rest[1], rest[2:]
        made = 1 if last else PARTS
        received, (*out, scaled) = rest[: -1 - made], rest[-1 - made :]
        degree = degrees.at[1 if last else 0]

    size = scaled.shape[0] // PARTS

    def add(b, carry, part=0):
        total = own[b]
        for piece in received:
            total = total + piece[b].astype(F32)
        total = total / degree[pl.ds(b, 1), :]
        if normalize:
            total = split_dot(inverse[...], total)
        scaled[b] = total
        if not last:
            out[part][b - part * size] = total.astype(BF16)
        return carry

    if last:
        lax.fori_loop(0, scaled.shape[0], add, 0, unroll=scaled.shape[0])
        out[0][...] = gram_of(scaled)
        return
    for part in range(PARTS):
        lax.fori_loop(part * size, (part + 1) * size, functools.partial(add, part=part), 0, unroll=size)


def split_dot(left, right):
    (left_high, left_low), (right_high, right_low) = two_parts(left), two_parts(right)
    both = jnp.concatenate([left_high, left_low], axis=0)
    upper = jnp.dot(both, right_high, preferred_element_type=F32)
    lower = jnp.dot(left_high, right_low, preferred_element_type=F32)
    return upper[: left.shape[0]] + (upper[left.shape[0] :] + lower)


def gram_of(scaled):
    features = scaled.shape[1]
    contract = (((1,), (1,)), ((), ()))
    with_first, second = jnp.zeros((3 * features, features), F32), jnp.zeros((features, features), F32)
    for b in range(scaled.shape[0]):
        value = scaled[b]
        high = value.astype(BF16)
        middle, low = two_parts(value - high.astype(F32))
        parts = jnp.concatenate([high, middle, low], axis=0)
        with_first = with_first + lax.dot_general(parts, high, contract, preferred_element_type=F32)
        second = second + lax.dot_general(middle, middle, contract, preferred_element_type=F32)
    cross = with_first[features : 2 * features] + with_first[2 * features :]
    return with_first[:features] + (cross + cross.T) + second


def gram_kernel(scaled, mark, gram):
    gram[...] = gram_of(scaled)


def inverse_factor(gram):
    size, step = gram.shape[0], 8
    row = lax.broadcasted_iota(jnp.int32, (size, size), 0)
    lane = lax.broadcasted_iota(jnp.int32, (size, size), 1)
    both = jnp.concatenate([gram, (row == lane).astype(F32)], axis=1)
    rows = [both[i : i + step] for i in range(0, size, step)]
    within = lax.broadcasted_iota(jnp.int32, rows[0].shape, 0)
    for p in range(len(rows)):
        cols = {
            i: [jnp.broadcast_to(rows[i][:, p * step + k : p * step + k + 1], rows[i].shape) for k in range(step)]
            for i in range(p, len(rows))
        }
        for k in range(step):
            pivot = [cols[p][l][k : k + 1] for l in range(step)]
            pivot_row = rows[p][k : k + 1]
            one = 1.0 / pivot[k]
            for i in range(p, len(rows)):
                scale = cols[i][k] * one
                if i == p:
                    scale = jnp.where(within > k, scale, 0.0)
                for l in range(k + 1, step):
                    cols[i][l] = cols[i][l] - scale * pivot[l]
                rows[i] = rows[i] - scale * pivot_row
    both = jnp.concatenate(rows, axis=0)
    pivots = jnp.sum(jnp.where(row == lane, both[:, :size], 0.0), axis=1, keepdims=True)
    return both[:, size:] * lax.rsqrt(pivots)


def factor_kernel(nodes, *refs):
    grams, inverse = refs[:-1], refs[-1]
    inverse[...] = inverse_factor(sum(g[...] for g in grams) / nodes)


def final_kernel(nodes, scaled, *refs):
    grams, out = refs[:-1], refs[-1]
    inverse = inverse_factor(sum(g[...] for g in grams) / nodes)
    tile = scaled.shape[2]
    for b in range(scaled.shape[0]):
        out[:, b * tile : (b + 1) * tile] = split_dot(inverse, scaled[b])


def params(limit=LIMIT):
    return pltpu.CompilerParams(vmem_limit_bytes=limit)


def chip_parts(gram):
    return [gram] + [exchange(gram, "col", d) for d in range(2, lax.axis_size("col"), 2)]


def along_row(gram):
    return [gram] + [exchange(gram, "row", d) for d in range(1, lax.axis_size("row"))]


def local(embed, tiles, tile_rows, tile_cols, chg_tiles, chg_rows, chg_cols):
    rows_dev, features = embed.shape
    tile = tiles.shape[1]
    row_size, col_size = lax.axis_size("row"), lax.axis_size("col")
    devices = row_size * col_size
    per_device = rows_dev // tile
    row_blocks, col_blocks = per_device * col_size, per_device * row_size
    sub = rows_dev // devices
    groups = tile // sub
    per_row = col_size // groups
    half = col_size // 2
    product_limit = 2 * (tiles.size + 3 * devices * CAP * tile * tile // 2 + 8 * row_blocks * features * tile) + 6 * MIB
    nodes = rows_dev * devices
    row, col = lax.axis_index("row"), lax.axis_index("col")
    chip = (col // 2).reshape(1)
    block = jax.ShapeDtypeStruct((per_device, features, tile), BF16)
    block32 = jax.ShapeDtypeStruct((per_device, features, tile), F32)

    member, family = col % groups, col // groups
    embed_t = embed.T
    early = [d for d in range(row_size) if d & (d - 1) == 0]
    raw = [embed_t] + [exchange(embed_t, "row", d) for d in early[1:]]
    slots = pl.pallas_call(
        functools.partial(pack_kernel, devices, row_blocks, col_blocks, col_size),
        out_shape=jax.ShapeDtypeStruct((devices, CAP * tile + 16, tile), BF16),
        in_specs=[ANY, ANY, ANY],
        out_specs=VMEM,
        scratch_shapes=[
            pltpu.SMEM(chg_rows.shape, jnp.int32),
            pltpu.SMEM(chg_rows.shape, jnp.int32),
            pltpu.SMEM((devices * CAP * 2,), jnp.int32),
            pltpu.SMEM((devices,), jnp.int32),
            pltpu.SemaphoreType.DMA((3,)),
        ],
        compiler_params=params(BIG),
        cost_estimate=NONE,
        name="pack",
    )(chg_rows, chg_cols, chg_tiles)
    merged = pl.pallas_call(
        functools.partial(merge_kernel, len(early), row_size, sub),
        out_shape=(jax.ShapeDtypeStruct((len(early) * row_size, features, tile), BF16),) * per_row,
        in_specs=[SMEM] + [VMEM] * (len(early) * groups),
        out_specs=(VMEM,) * per_row,
        compiler_params=params(2 * rows_dev * features * len(early) * (groups + row_size) + 8 * MIB),
        cost_estimate=NONE,
        name="merge",
    )(
        col.reshape(1),
        *[piece if d == 0 else exchange(piece, "col", d) for piece in raw for d in range(groups)],
    )
    gathered = [merged[0]] + [exchange(merged[d], "col", d * groups) for d in range(1, per_row)]
    complete = {}
    for d in range(1, row_size):
        if d in early:
            at = early.index(d) * row_size
            complete[d] = jnp.concatenate([piece[at : at + row_size] for piece in gathered], axis=0)
        else:
            complete[d] = exchange(complete[d & (d - 1)], "row", d & -d)
    late = [complete[d] for d in range(row_size) if d not in early]
    slots = lax.optimization_barrier((slots, *raw[1:]))[0]
    taken = lax.all_to_all(slots, ("row", "col"), split_axis=0, concat_axis=0, tiled=True)

    def x_block(position, first):
        source = position % per_device // per_row
        outer, inner = position // per_device, position % per_row
        if first:
            return (jnp.bitwise_xor(source, row) * per_row + jnp.bitwise_xor(inner, family)) * row_size + outer
        return jnp.bitwise_xor(source, row) * per_device + outer * per_row + inner

    own_rows, own_cols = tile_rows % row_blocks, tile_cols % col_blocks
    per_tile = tile // features
    stock_blocks = tiles.shape[0] * per_tile + col_blocks + 2 * row_blocks // features
    stock = pl.pallas_call(
        functools.partial(stock_kernel, early, row_size),
        out_shape=jax.ShapeDtypeStruct((stock_blocks, features, tile), BF16),
        in_specs=[SMEM] + [VMEM] * (1 + len(gathered) + len(late)),
        out_specs=VMEM,
        scratch_shapes=[pltpu.VMEM((row_blocks, tile), F32)],
        compiler_params=params(4 * tiles.size + 4 * stock_blocks * features * tile + 4 * MIB),
        cost_estimate=NONE,
        name="stock",
    )(own_rows, tiles, *gathered, *late)

    place = jnp.stack([col % 2, family, row])
    square = jax.ShapeDtypeStruct((features, features), F32)
    numbers_shape = jax.ShapeDtypeStruct((devices, tile), jnp.int32)
    for iteration in range(ITERS):
        first, last = iteration == 0, iteration == ITERS - 1
        blocks = per_device + 1 if first else per_device
        shape = (blocks, features, tile)
        if iteration:
            gathered = {0: current}
            for d in sorted(range(1, row_size), key=lambda d: (d & (d - 1) != 0, -d if d & (d - 1) == 0 else d)):
                low = d & -d
                gathered[d] = [exchange(part, "row", low) for part in gathered[d ^ low]]
            first_part = gathered[row_size // 2][0]
            gathered = [part for d in range(row_size) for part in gathered[d]]
            gram = pl.pallas_call(
                gram_kernel,
                out_shape=jax.ShapeDtypeStruct((features, features), F32),
                in_specs=[VMEM, VMEM],
                out_specs=VMEM,
                compiler_params=params(),
                cost_estimate=NONE,
                name="gram",
            )(scaled, first_part)
            grams = chip_parts(gram + exchange(gram, "col", 1))
        keep, send, found = pl.pallas_call(
            functools.partial(product_kernel, not last, first, sub, per_device, row_size, half, 0 if first else len(gathered)),
            out_shape=(jax.ShapeDtypeStruct((half, *shape), BF16),) * 2 + (numbers_shape if first else square,),
            in_specs=[SMEM] * 3 + ([VMEM] * 2 if first else [SMEM] + [VMEM] * (2 + half + len(gathered))),
            out_specs=(VMEM, VMEM, VMEM),
            scratch_shapes=[
                pltpu.VMEM((1 if first else col_blocks, features, tile), BF16),
                pltpu.VMEM((row_blocks, features, tile), F32),
                pltpu.VMEM((row_blocks, tile), F32),
                pltpu.VMEM((per_device, tile), F32),
            ] + first * [
                pltpu.VMEM((devices, tile), jnp.int32),
                pltpu.SMEM((devices, tile), jnp.int32),
                pltpu.SemaphoreType.DMA,
            ],
            compiler_params=params(product_limit),
            cost_estimate=NONE,
            name="product",
        )(
            place, own_rows, x_block(own_cols, first),
            *([] if first else [numbers, *grams]), stock, taken, *([] if first else gathered),
        )
        other = exchange(send, "col", 1)
        if iteration:
            grams = along_row(found)
        else:
            numbers = found
        paired = pl.pallas_call(
            functools.partial(pair_kernel, per_device),
            out_shape=(jax.ShapeDtypeStruct(shape, BF16),) * (half - 1) + (jax.ShapeDtypeStruct(shape, F32),),
            in_specs=[SMEM, VMEM, VMEM],
            out_specs=(VMEM,) * half,
            compiler_params=params(),
            cost_estimate=NONE,
            name="pair",
        )(chip, keep, other)
        received = [exchange(piece, "col", 2 * (i + 1)) for i, piece in enumerate(paired[:-1])]
        if iteration:
            inverse = pl.pallas_call(
                functools.partial(factor_kernel, nodes),
                out_shape=jax.ShapeDtypeStruct((features, features), F32),
                in_specs=[VMEM] * len(grams),
                out_specs=VMEM,
                compiler_params=params(),
                cost_estimate=NONE,
                name="factor",
            )(*grams)
        both = jax.ShapeDtypeStruct((2, per_device, tile), F32)
        piece = jax.ShapeDtypeStruct((per_device // PARTS, features, tile), BF16)
        *current, scaled = pl.pallas_call(
            functools.partial(scale_kernel, not first, last, first),
            out_shape=((square,) if last else (piece,) * PARTS) + (block32,) + ((both,) if first else ()),
            in_specs=[VMEM] * ((1 if first else 3) + half - 1),
            out_specs=(VMEM,) * (2 if last else PARTS + 2 if first else PARTS + 1),
            compiler_params=params(),
            cost_estimate=NONE,
            name="scale",
        )(paired[-1], *([] if first else [degrees, inverse]), *received)
        if first:
            *current, scaled, degrees = *current, scaled
    out = pl.pallas_call(
        functools.partial(final_kernel, nodes),
        out_shape=jax.ShapeDtypeStruct((features, rows_dev), F32),
        in_specs=[VMEM] * (1 + row_size),
        out_specs=VMEM,
        compiler_params=params(),
        cost_estimate=NONE,
        name="final",
    )(scaled, *along_row(sum(chip_parts(current[0] + exchange(current[0], "col", 1)))))
    return out.T


def solution(mesh):
    placed = (
        P(("row", "col"), None),
        P(("row", "col"), None, None),
        P(("row", "col")),
        P(("row", "col")),
        P(("row", "col"), None, None),
        P(("row", "col")),
        P(("row", "col")),
    )
    return jax.shard_map(
        local, mesh=mesh, in_specs=placed, out_specs=P(("row", "col"), None), check_vma=False
    )
```

```python
import functools

import jax
import jax.numpy as jnp
from jax import lax
from jax.experimental import pallas as pl
from jax.experimental.pallas import tpu as pltpu
from jax.sharding import PartitionSpec as P

ITERS = 3
CAP = 3
PARTS = 2
F32 = jnp.float32
BF16 = jnp.bfloat16
VMEM = pl.BlockSpec(memory_space=pltpu.VMEM)
SMEM = pl.BlockSpec(memory_space=pltpu.SMEM)
ANY = pl.BlockSpec(memory_space=pl.ANY)
MIB = 1024 * 1024
LIMIT = 12 * MIB
BIG = 60 * MIB
NONE = pl.CostEstimate(flops=0, bytes_accessed=0, transcendentals=0)


def exchange(value, axis, distance):
    size = lax.axis_size(axis)
    return lax.ppermute(value, axis, [(i, i ^ distance) for i in range(size)])


def pack_kernel(devices, row_blocks, col_blocks, col_count, rows_in, cols_in, chg, slots, rows, cols, places, counts, sems):
    listed, tile = chg.shape[:2]
    loads = [pltpu.make_async_copy(rows_in, rows, sems.at[0]), pltpu.make_async_copy(cols_in, cols, sems.at[1])]
    for load in loads:
        load.start()

    def clear(i, carry):
        slots[i] = jnp.zeros(slots.shape[1:], slots.dtype)
        counts[i] = 0
        for k in range(2 * CAP):
            places[2 * CAP * i + k] = 0
        return carry

    lax.fori_loop(0, devices, clear, 0)
    for load in loads:
        load.wait()

    def place(i, carry):
        row, col = cols[i], rows[i]
        owner = lax.div(row, row_blocks) * col_count + lax.div(col, col_blocks)
        rank = counts[owner]
        counts[owner] = rank + 1
        at = 2 * (owner * CAP + rank)
        places[at] = lax.rem(row, row_blocks)
        places[at + 1] = lax.rem(col, col_blocks)
        there = pl.ds(pl.multiple_of(rank * tile, tile), tile)
        pltpu.make_async_copy(chg.at[i], slots.at[owner, there], sems.at[2]).start()
        return carry

    lax.fori_loop(0, listed, place, 0, unroll=4)
    pltpu.make_async_copy(chg, chg, sems.at[2]).wait()
    lane = lax.broadcasted_iota(jnp.int32, (16, tile), 1)

    def note(i, carry):
        value = jnp.zeros(lane.shape, jnp.int32)
        for k in range(2 * CAP):
            value = jnp.where(lane == k, places[2 * CAP * i + k], value)
        slots[i, CAP * tile :] = value.astype(F32).astype(BF16)
        return carry

    lax.fori_loop(0, devices, note, 0, unroll=2)


def stock_kernel(early, row_size, tile_rows, tiles, *refs):
    pieces, (stock, degree) = refs[:-2], refs[-2:]
    tile, count = tiles.shape[1], tiles.shape[0]
    features = stock.shape[1]
    per_tile = tile // features
    degree[...] = jnp.zeros(degree.shape, F32)

    def own(i, carry):
        value = tiles[i].T
        for k in range(per_tile):
            stock[i * per_tile + k] = value[k * features : (k + 1) * features]
        degree[pl.ds(tile_rows[i], 1), :] += jnp.sum(jnp.abs(value.astype(F32)), axis=0, keepdims=True)
        return carry

    lax.fori_loop(0, count, own, 0, unroll=4)
    at = count * per_tile
    families = len(pieces) - (row_size - len(early))
    late = list(pieces[families:])
    for d in range(row_size):
        if d in early:
            start = early.index(d) * row_size
            for family in range(families):
                stock[at : at + row_size] = pieces[family][start : start + row_size]
                at += row_size
        else:
            piece = late.pop(0)
            stock[at : at + piece.shape[0]] = piece[...]
            at += piece.shape[0]
    high, low = two_parts(degree[...])
    for part in (high, low):
        for k in range(0, part.shape[0], features):
            stock[at] = part[k : k + features]
            at += 1


def two_parts(value):
    high = value.astype(BF16)
    return high, (value - high.astype(F32)).astype(BF16)


def one_part(block, at, rows):
    return block[at : at + rows].astype(F32) + block[at + rows : at + 2 * rows].astype(F32)


def merge_kernel(count, row_size, sub, place, *refs):
    features, tile = refs[-1].shape[1:]
    groups = tile // sub
    sources, outs = refs[: count * groups], refs[count * groups :]
    member, family = place[0] % groups, place[0] // groups
    lane = lax.broadcasted_iota(jnp.int32, (features, tile), 1) // sub
    for distance, out in enumerate(outs):
        for source in range(count):

            def join(r, carry, distance=distance, out=out, source=source):
                block = r * len(outs) + jnp.bitwise_xor(family, distance)
                at = pl.ds(pl.multiple_of(block * tile, tile), tile)
                value = sources[source * groups][:, at].astype(F32)
                for d in range(1, groups):
                    g = jnp.bitwise_xor(member, d)
                    moved = pltpu.roll(sources[source * groups + d][:, at].astype(F32), (g - member) * sub % tile, 1)
                    value = jnp.where(lane == g, moved, value)
                out[source * row_size + r] = value.astype(BF16)
                return carry

            lax.fori_loop(0, row_size, join, 0, unroll=4)


def product_kernel(by_column, first, sub, per_device, row_size, chips, held, place, own_rows, own_x, *rest):
    if not first:
        numbers, grams, rest = rest[0], rest[1 : 1 + chips], rest[1 + chips :]
    stock, taken, rest = rest[0], rest[1], rest[2:]
    pieces, outs, found, scratch = rest[:held], rest[held : held + 2], rest[held + 2], rest[held + 3 :]
    x_buf, total, degree, part_buf = scratch[:4]
    half, (features, tile) = outs[0].shape[0], stock.shape[1:]
    per_tile = tile // features
    tile_count = own_rows.shape[0]
    groups = tile // sub
    per_row = 2 * half // groups
    total[...] = jnp.zeros(total.shape, F32)
    if first:
        number_buf, numbers, sems = scratch[4:]
        x_start, x_blocks = tile_count * per_tile, per_device * row_size
        parts, rows = stock.shape[0] - (x_start + x_blocks), degree.shape[0]
        own_degree = stock[x_start + x_blocks :].reshape(parts * features, tile).astype(F32)
        degree[...] = own_degree[:rows] + own_degree[rows:]
        note = taken[:, CAP * tile :].astype(F32)[:, 0, :].astype(jnp.int32)
        lane = lax.broadcasted_iota(jnp.int32, note.shape, 1)
        per_row_bits, per_device_bits = per_row.bit_length() - 1, per_device.bit_length() - 1
        inner, outer = jnp.bitwise_and(note, per_row - 1), jnp.right_shift(note, per_device_bits)
        source = jnp.bitwise_xor(jnp.right_shift(jnp.bitwise_and(note, per_device - 1), per_row_bits), place[2])
        block = (source * per_row + jnp.bitwise_xor(inner, place[1])) * row_size + outer
        even = jnp.bitwise_and(lane, 1) == 0
        number_buf[...] = jnp.where(even, note, block)
        found[...] = jnp.where(even, note, source * per_device + outer * per_row + inner)
        numbers_copy = pltpu.make_async_copy(number_buf, numbers, sems)
        numbers_copy.start()
    else:
        found[...] = sum(gram[...] for gram in grams)
        size = per_device // PARTS
        for i, piece in enumerate(pieces):
            x_buf[i * size : (i + 1) * size] = piece[...]

    def x_block(block):
        return stock[x_start + block] if first else x_buf[block]

    def add_own(i, carry):
        value = stock[pl.ds(i * per_tile, per_tile)].reshape(tile, tile)
        total[own_rows[i]] += jnp.dot(x_block(own_x[i]), value, preferred_element_type=F32)
        return carry

    lax.fori_loop(0, tile_count, add_own, 0, unroll=32 if first else 64)
    if first:
        numbers_copy.wait()

    def add_taken(i, carry):
        for k in range(CAP):
            row, block = numbers[i, 2 * k], numbers[i, 2 * k + 1]
            value = taken[i, k * tile : (k + 1) * tile]
            if first:
                degree[pl.ds(row, 1), :] += jnp.sum(jnp.abs(value.astype(F32)), axis=0, keepdims=True)
            total[row] += jnp.dot(x_block(block), value, preferred_element_type=F32)
        return carry

    lax.fori_loop(0, taken.shape[0], add_taken, 0, unroll=8 if first else 32)

    def write(mine):
        lane = lax.broadcasted_iota(jnp.int32, total.shape[1:], 1) // sub

        def regroup(r, carry):
            for part in range(per_row):
                for j in range(per_row):
                    base = j * groups * per_device + part + r * per_row
                    blocks = [total[base + g * per_device] for g in range(groups)]
                    for side in range(groups):
                        column = part * groups + side
                        value = blocks[0]
                        for g in range(groups):
                            shift = (g - side) * sub % tile
                            moved = pltpu.roll(blocks[g], shift, 1) if shift else blocks[g]
                            value = moved if g == 0 else jnp.where(lane == g, moved, value)
                        outs[(column + mine) % 2][column // 2, r * per_row + j] = value.astype(BF16)
            return carry

        def straight(i, carry):
            for column in range(2 * half):
                outs[(column + mine) % 2][column // 2, i] = total[column * per_device + i].astype(BF16)
            return carry

        if by_column:
            lax.fori_loop(0, row_size, regroup, 0, unroll=row_size)
        else:
            lax.fori_loop(0, per_device, straight, 0, unroll=8)
        if not first:
            return
        lane = lax.broadcasted_iota(jnp.int32, (row_size, tile), 1) // sub
        for column in range(2 * half):
            part, side = column // groups, column % groups
            for j in range(per_row):
                value = None
                for g in range(groups):
                    block = degree[pl.ds((j * groups + g) * per_device + part, row_size, stride=per_row), :]
                    shift = (g - side) * sub % tile
                    moved = pltpu.roll(block, shift, 1) if shift else block
                    value = moved if g == 0 else jnp.where(lane == g, moved, value)
                part_buf[pl.ds(j, row_size, stride=per_row), :] = value
            by_node = degree[column * per_device : (column + 1) * per_device, :]
            values = two_parts(part_buf[...]) + two_parts(by_node)
            outs[(column + mine) % 2][column // 2, per_device] = jnp.concatenate(values, axis=0)

    for mine in range(2):
        pl.when(place[0] == mine)(functools.partial(write, mine))


def pair_kernel(per_device, chip, keep, other, *out):
    for i, piece in enumerate(out):
        there = jnp.bitwise_xor(chip[0], (i + 1) % len(out))

        def add(b, carry, piece=piece, there=there):
            piece[b] = (keep[there, b].astype(F32) + other[there, b].astype(F32)).astype(piece.dtype)
            return carry

        lax.fori_loop(0, per_device, add, 0, unroll=4)
        if piece.shape[0] > per_device:
            here, sent = keep[there, per_device], other[there, per_device]
            for at in (0, 2 * per_device):
                value = one_part(here, at, per_device) + one_part(sent, at, per_device)
                high, low = two_parts(value)
                piece[per_device, at : at + per_device] = high.astype(piece.dtype)
                piece[per_device, at + per_device : at + 2 * per_device] = low.astype(piece.dtype)


def scale_kernel(normalize, last, first, own, *rest):
    if first:
        received, (*out, scaled, degrees) = rest[: -2 - PARTS], rest[-2 - PARTS :]
        per_device = scaled.shape[0]
        parts = [own[per_device]] + [piece[per_device] for piece in received]
        for i in range(2):
            degrees[i] = 1.0 + sum(one_part(part, 2 * i * per_device, per_device) for part in parts)
        degree = degrees.at[0]
    else:
        degrees, inverse, rest = rest[0], rest[1], rest[2:]
        made = 1 if last else PARTS
        received, (*out, scaled) = rest[: -1 - made], rest[-1 - made :]
        degree = degrees.at[1 if last else 0]

    size = scaled.shape[0] // PARTS

    def add(b, carry, part=0):
        total = own[b]
        for piece in received:
            total = total + piece[b].astype(F32)
        total = total / degree[pl.ds(b, 1), :]
        if normalize:
            total = split_dot(inverse[...], total)
        scaled[b] = total
        if not last:
            out[part][b - part * size] = total.astype(BF16)
        return carry

    if last:
        lax.fori_loop(0, scaled.shape[0], add, 0, unroll=scaled.shape[0])
        out[0][...] = gram_of(scaled)
        return
    for part in range(PARTS):
        lax.fori_loop(part * size, (part + 1) * size, functools.partial(add, part=part), 0, unroll=size)


def split_dot(left, right):
    (left_high, left_low), (right_high, right_low) = two_parts(left), two_parts(right)
    both = jnp.concatenate([left_high, left_low], axis=0)
    upper = jnp.dot(both, right_high, preferred_element_type=F32)
    lower = jnp.dot(left_high, right_low, preferred_element_type=F32)
    return upper[: left.shape[0]] + (upper[left.shape[0] :] + lower)


def gram_of(scaled):
    features = scaled.shape[1]
    contract = (((1,), (1,)), ((), ()))
    with_first, second = jnp.zeros((3 * features, features), F32), jnp.zeros((features, features), F32)
    for b in range(scaled.shape[0]):
        value = scaled[b]
        high = value.astype(BF16)
        middle, low = two_parts(value - high.astype(F32))
        parts = jnp.concatenate([high, middle, low], axis=0)
        with_first = with_first + lax.dot_general(parts, high, contract, preferred_element_type=F32)
        second = second + lax.dot_general(middle, middle, contract, preferred_element_type=F32)
    cross = with_first[features : 2 * features] + with_first[2 * features :]
    return with_first[:features] + (cross + cross.T) + second


def gram_kernel(scaled, mark, gram):
    gram[...] = gram_of(scaled)


def inverse_factor(gram):
    size, step = gram.shape[0], 8
    row = lax.broadcasted_iota(jnp.int32, (size, size), 0)
    lane = lax.broadcasted_iota(jnp.int32, (size, size), 1)
    both = jnp.concatenate([gram, (row == lane).astype(F32)], axis=1)
    rows = [both[i : i + step] for i in range(0, size, step)]
    within = lax.broadcasted_iota(jnp.int32, rows[0].shape, 0)
    for p in range(len(rows)):
        cols = {
            i: [jnp.broadcast_to(rows[i][:, p * step + k : p * step + k + 1], rows[i].shape) for k in range(step)]
            for i in range(p, len(rows))
        }
        for k in range(step):
            pivot = [cols[p][l][k : k + 1] for l in range(step)]
            pivot_row = rows[p][k : k + 1]
            one = 1.0 / pivot[k]
            for i in range(p, len(rows)):
                scale = cols[i][k] * one
                if i == p:
                    scale = jnp.where(within > k, scale, 0.0)
                for l in range(k + 1, step):
                    cols[i][l] = cols[i][l] - scale * pivot[l]
                rows[i] = rows[i] - scale * pivot_row
    both = jnp.concatenate(rows, axis=0)
    pivots = jnp.sum(jnp.where(row == lane, both[:, :size], 0.0), axis=1, keepdims=True)
    return both[:, size:] * lax.rsqrt(pivots)


def factor_kernel(nodes, *refs):
    grams, inverse = refs[:-1], refs[-1]
    inverse[...] = inverse_factor(sum(g[...] for g in grams) / nodes)


def final_kernel(nodes, scaled, *refs):
    grams, out = refs[:-1], refs[-1]
    inverse = inverse_factor(sum(g[...] for g in grams) / nodes)
    tile = scaled.shape[2]
    for b in range(scaled.shape[0]):
        out[:, b * tile : (b + 1) * tile] = split_dot(inverse, scaled[b])


def params(limit=LIMIT):
    return pltpu.CompilerParams(vmem_limit_bytes=limit)


def chip_parts(gram):
    return [gram] + [exchange(gram, "col", d) for d in range(2, lax.axis_size("col"), 2)]


def along_row(gram):
    return [gram] + [exchange(gram, "row", d) for d in range(1, lax.axis_size("row"))]


def local(embed, tiles, tile_rows, tile_cols, chg_tiles, chg_rows, chg_cols):
    rows_dev, features = embed.shape
    tile = tiles.shape[1]
    row_size, col_size = lax.axis_size("row"), lax.axis_size("col")
    devices = row_size * col_size
    per_device = rows_dev // tile
    row_blocks, col_blocks = per_device * col_size, per_device * row_size
    sub = rows_dev // devices
    groups = tile // sub
    per_row = col_size // groups
    half = col_size // 2
    product_limit = 2 * (tiles.size + 3 * devices * CAP * tile * tile // 2 + 8 * row_blocks * features * tile) + 6 * MIB
    nodes = rows_dev * devices
    row, col = lax.axis_index("row"), lax.axis_index("col")
    chip = (col // 2).reshape(1)
    block = jax.ShapeDtypeStruct((per_device, features, tile), BF16)
    block32 = jax.ShapeDtypeStruct((per_device, features, tile), F32)

    member, family = col % groups, col // groups
    embed_t = embed.T
    early = [d for d in range(row_size) if d & (d - 1) == 0]
    raw = [embed_t] + [exchange(embed_t, "row", d) for d in early[1:]]
    slots = pl.pallas_call(
        functools.partial(pack_kernel, devices, row_blocks, col_blocks, col_size),
        out_shape=jax.ShapeDtypeStruct((devices, CAP * tile + 16, tile), BF16),
        in_specs=[ANY, ANY, ANY],
        out_specs=VMEM,
        scratch_shapes=[
            pltpu.SMEM(chg_rows.shape, jnp.int32),
            pltpu.SMEM(chg_rows.shape, jnp.int32),
            pltpu.SMEM((devices * CAP * 2,), jnp.int32),
            pltpu.SMEM((devices,), jnp.int32),
            pltpu.SemaphoreType.DMA((3,)),
        ],
        compiler_params=params(BIG),
        cost_estimate=NONE,
        name="pack",
    )(chg_rows, chg_cols, chg_tiles)
    merged = pl.pallas_call(
        functools.partial(merge_kernel, len(early), row_size, sub),
        out_shape=(jax.ShapeDtypeStruct((len(early) * row_size, features, tile), BF16),) * per_row,
        in_specs=[SMEM] + [VMEM] * (len(early) * groups),
        out_specs=(VMEM,) * per_row,
        compiler_params=params(2 * rows_dev * features * len(early) * (groups + row_size) + 8 * MIB),
        cost_estimate=NONE,
        name="merge",
    )(
        col.reshape(1),
        *[piece if d == 0 else exchange(piece, "col", d) for piece in raw for d in range(groups)],
    )
    gathered = [merged[0]] + [exchange(merged[d], "col", d * groups) for d in range(1, per_row)]
    complete = {}
    for d in range(1, row_size):
        if d in early:
            at = early.index(d) * row_size
            complete[d] = jnp.concatenate([piece[at : at + row_size] for piece in gathered], axis=0)
        else:
            complete[d] = exchange(complete[d & (d - 1)], "row", d & -d)
    late = [complete[d] for d in range(row_size) if d not in early]
    slots = lax.optimization_barrier((slots, *raw[1:]))[0]
    taken = lax.all_to_all(slots, ("row", "col"), split_axis=0, concat_axis=0, tiled=True)

    def x_block(position, first):
        source = position % per_device // per_row
        outer, inner = position // per_device, position % per_row
        if first:
            return (jnp.bitwise_xor(source, row) * per_row + jnp.bitwise_xor(inner, family)) * row_size + outer
        return jnp.bitwise_xor(source, row) * per_device + outer * per_row + inner

    own_rows, own_cols = tile_rows % row_blocks, tile_cols % col_blocks
    per_tile = tile // features
    stock_blocks = tiles.shape[0] * per_tile + col_blocks + 2 * row_blocks // features
    stock = pl.pallas_call(
        functools.partial(stock_kernel, early, row_size),
        out_shape=jax.ShapeDtypeStruct((stock_blocks, features, tile), BF16),
        in_specs=[SMEM] + [VMEM] * (1 + len(gathered) + len(late)),
        out_specs=VMEM,
        scratch_shapes=[pltpu.VMEM((row_blocks, tile), F32)],
        compiler_params=params(4 * tiles.size + 4 * stock_blocks * features * tile + 4 * MIB),
        cost_estimate=NONE,
        name="stock",
    )(own_rows, tiles, *gathered, *late)

    place = jnp.stack([col % 2, family, row])
    square = jax.ShapeDtypeStruct((features, features), F32)
    numbers_shape = jax.ShapeDtypeStruct((devices, tile), jnp.int32)
    for iteration in range(ITERS):
        first, last = iteration == 0, iteration == ITERS - 1
        blocks = per_device + 1 if first else per_device
        shape = (blocks, features, tile)
        if iteration:
            gathered = {0: current}
            for d in sorted(range(1, row_size), key=lambda d: (d & (d - 1) != 0, -d if d & (d - 1) == 0 else d)):
                low = d & -d
                gathered[d] = [exchange(part, "row", low) for part in gathered[d ^ low]]
            first_part = gathered[row_size // 2][0]
            gathered = [part for d in range(row_size) for part in gathered[d]]
            gram = pl.pallas_call(
                gram_kernel,
                out_shape=jax.ShapeDtypeStruct((features, features), F32),
                in_specs=[VMEM, VMEM],
                out_specs=VMEM,
                compiler_params=params(),
                cost_estimate=NONE,
                name="gram",
            )(scaled, first_part)
            grams = chip_parts(gram + exchange(gram, "col", 1))
        keep, send, found = pl.pallas_call(
            functools.partial(product_kernel, not last, first, sub, per_device, row_size, half, 0 if first else len(gathered)),
            out_shape=(jax.ShapeDtypeStruct((half, *shape), BF16),) * 2 + (numbers_shape if first else square,),
            in_specs=[SMEM] * 3 + ([VMEM] * 2 if first else [SMEM] + [VMEM] * (2 + half + len(gathered))),
            out_specs=(VMEM, VMEM, VMEM),
            scratch_shapes=[
                pltpu.VMEM((1 if first else col_blocks, features, tile), BF16),
                pltpu.VMEM((row_blocks, features, tile), F32),
                pltpu.VMEM((row_blocks, tile), F32),
                pltpu.VMEM((per_device, tile), F32),
            ] + first * [
                pltpu.VMEM((devices, tile), jnp.int32),
                pltpu.SMEM((devices, tile), jnp.int32),
                pltpu.SemaphoreType.DMA,
            ],
            compiler_params=params(product_limit),
            cost_estimate=NONE,
            name="product",
        )(
            place, own_rows, x_block(own_cols, first),
            *([] if first else [numbers, *grams]), stock, taken, *([] if first else gathered),
        )
        other = exchange(send, "col", 1)
        if iteration:
            grams = along_row(found)
        else:
            numbers = found
        paired = pl.pallas_call(
            functools.partial(pair_kernel, per_device),
            out_shape=(jax.ShapeDtypeStruct(shape, BF16),) * (half - 1) + (jax.ShapeDtypeStruct(shape, F32),),
            in_specs=[SMEM, VMEM, VMEM],
            out_specs=(VMEM,) * half,
            compiler_params=params(),
            cost_estimate=NONE,
            name="pair",
        )(chip, keep, other)
        received = [exchange(piece, "col", 2 * (i + 1)) for i, piece in enumerate(paired[:-1])]
        if iteration:
            inverse = pl.pallas_call(
                functools.partial(factor_kernel, nodes),
                out_shape=jax.ShapeDtypeStruct((features, features), F32),
                in_specs=[VMEM] * len(grams),
                out_specs=VMEM,
                compiler_params=params(),
                cost_estimate=NONE,
                name="factor",
            )(*grams)
        both = jax.ShapeDtypeStruct((2, per_device, tile), F32)
        piece = jax.ShapeDtypeStruct((per_device // PARTS, features, tile), BF16)
        *current, scaled = pl.pallas_call(
            functools.partial(scale_kernel, not first, last, first),
            out_shape=((square,) if last else (piece,) * PARTS) + (block32,) + ((both,) if first else ()),
            in_specs=[VMEM] * ((1 if first else 3) + half - 1),
            out_specs=(VMEM,) * (2 if last else PARTS + 2 if first else PARTS + 1),
            compiler_params=params(),
            cost_estimate=NONE,
            name="scale",
        )(paired[-1], *([] if first else [degrees, inverse]), *received)
        if first:
            *current, scaled, degrees = *current, scaled
    out = pl.pallas_call(
        functools.partial(final_kernel, nodes),
        out_shape=jax.ShapeDtypeStruct((features, rows_dev), F32),
        in_specs=[VMEM] * (1 + row_size),
        out_specs=VMEM,
        compiler_params=params(),
        cost_estimate=NONE,
        name="final",
    )(scaled, *along_row(sum(chip_parts(current[0] + exchange(current[0], "col", 1)))))
    return out.T


def solution(mesh):
    placed = (
        P(("row", "col"), None),
        P(("row", "col"), None, None),
        P(("row", "col")),
        P(("row", "col")),
        P(("row", "col"), None, None),
        P(("row", "col")),
        P(("row", "col")),
    )
    return jax.shard_map(
        local, mesh=mesh, in_specs=placed, out_specs=P(("row", "col"), None), check_vma=False
    )
```
